256 devices in a mesh: row: 64 (over z, y, core), col: 4 (over x).
Axes of the slice: x: 4, y: 4, z: 8, core: 2. Of those that a mesh axis runs over, the one named last changes fastest.
Arguments:
- density_panel: bfloat16 [32768, 256], P('row'), may hold values from -6 to 6
- blocks: bfloat16 [98304, 4096], P(('row', 'col')), may hold values from -0.0625 to 0.0625
- block_row: int32 [98304], P(('row', 'col')), may hold values from 0 to 7
- block_slot: int32 [98304], P(('row', 'col')), may hold values from -1 to 127, as said below
- requests: int32 [16384, 2], P(('row', 'col')), may hold values from -1 to 7, as said below
Outputs:
- first_product: bfloat16 [32768, 256], P('row')
- second_product: bfloat16 [32768, 256], P('row')
The draws below stay inside these ranges and needn't reach their ends.
Inputs may be any that keep to these rules, and one draw needn't show every extreme that they name: requests[d * 64 + o, t] is -1 or t * 4 + d % 4; it is -1 whenever o < d // 4 and never when o = d // 4. A live block's slot holds a request other than -1, bi <= bj, and no two live blocks of one list share both block_row and block_slot.
All inputs are finite; a program needn't handle non-finite values.
Results may differ from the reference program's by a relative error of at most 0.0039.
Values may be sent and summed in bfloat16 or wider, within the bound.
A program may use at most 128 MiB of HBM per device.

```python
import jax
import jax.numpy as jnp
from jax import lax

B = 64
K = 256
GROUP_BLOCK_ROWS = 8
NBLK_DEV = 384
OWNERS = 64
SPLIT = 4
LISTS = 256
CAP = 2
SLOTS_PER_LIST = 128
POSITIONS = 1024
BLOCKROWS = 512


def shuffle_one(subkey):
    return jax.random.permutation(subkey, POSITIONS)


def pattern(key):
    device = jnp.arange(LISTS, dtype=jnp.int32)
    group = device // SPLIT
    column = device % SPLIT
    owner_index = jnp.arange(OWNERS, dtype=jnp.int32)
    within = jnp.arange(CAP, dtype=jnp.int32)
    local_index = within[None, None, :] * SPLIT + column[:, None, None]
    chance = jax.random.randint(jax.random.fold_in(key, 11), (LISTS, OWNERS, CAP), 0, 20)
    allowed = owner_index[None, :, None] >= group[:, None, None]
    own_group = owner_index[None, :, None] == group[:, None, None]
    last_group = owner_index[None, :, None] == OWNERS - 1
    used = allowed & ((chance < 17) | own_group | last_group)
    wanted = jnp.where(used, local_index, -1).astype(jnp.int32)
    subkeys = jax.random.split(jax.random.fold_in(key, 12), LISTS)
    shuffled = jax.vmap(shuffle_one)(subkeys)[:, :NBLK_DEV].astype(jnp.int32)
    target = SLOTS_PER_LIST * GROUP_BLOCK_ROWS - 1
    offset = (target - shuffled[:, :1]) % POSITIONS
    sorted_positions = ((shuffled + offset) % POSITIONS).astype(jnp.int32)
    chosen_slot = sorted_positions // GROUP_BLOCK_ROWS
    row_pick = sorted_positions % GROUP_BLOCK_ROWS
    within_bounds = sorted_positions < SLOTS_PER_LIST * GROUP_BLOCK_ROWS
    clamped_slot = jnp.minimum(chosen_slot, SLOTS_PER_LIST - 1)
    slot_owner = clamped_slot // CAP
    slot_within = clamped_slot % CAP
    needed = wanted[device[:, None], slot_owner, slot_within]
    valid = within_bounds & (needed >= 0) & ((slot_owner > group[:, None]) | (row_pick <= needed))
    block_slot = jnp.where(valid, clamped_slot, -1).astype(jnp.int32)
    return (wanted.reshape(LISTS * OWNERS, CAP), row_pick.reshape(-1).astype(jnp.int32), block_slot.reshape(-1))


def draw_requests(key, part):
    return pattern(key)[0]


def draw_block_row(key, part):
    return pattern(key)[1]


def draw_block_slot(key, part):
    return pattern(key)[2]


def block_levels(key, dims, shards, smallest, high):
    level, own = 1.0, jax.random.fold_in(key, 6)
    for dim, parts in shards:
        draws = jnp.exp(jax.random.uniform(jax.random.fold_in(own, dim), (parts,), jnp.float32, smallest / len(shards), high / len(shards)))
        level = level * jnp.repeat(draws, dims[dim] // parts).reshape([-1 if axis == dim else 1 for axis in range(len(dims))])
    return level


def centred(key, extent, deviation, bound, cuts=(), held_as=jnp.bfloat16):
    result = jax.random.normal(key, extent, jnp.float32) * deviation
    if len(cuts) > 0:
        result = block_levels(key, extent, cuts, -0.22, 0.18) * result
    return jnp.clip(result, min=-bound, max=bound).astype(held_as)


def setup_inputs(seed: int = 0) -> dict:
    seeds = jax.random.split(jax.random.key(seed), 6)
    return {
        "density_panel": centred(seeds[0], (BLOCKROWS * B, K), 1.0, 6.0, ((0, 64),)),
        "blocks": centred(seeds[1], (LISTS * NBLK_DEV, B * B), (B * 160) ** -0.5, 0.0625, ((0, 256),)),
        "block_row": draw_block_row(jax.random.fold_in(seeds[5], 71), 0),
        "block_slot": draw_block_slot(jax.random.fold_in(seeds[5], 71), 0),
        "requests": draw_requests(jax.random.fold_in(seeds[5], 71), 0),
    }


def apply_matrix(field, blocks, block_row, block_slot, requests):
    row_blocks = field.reshape(BLOCKROWS, B, K).astype(jnp.float32)

    def visit_list(summed, device):
        leading_block = device * NBLK_DEV
        pieces = lax.dynamic_slice_in_dim(blocks, leading_block, NBLK_DEV, 0).reshape(NBLK_DEV, B, B).astype(jnp.float32)
        rows_here = lax.dynamic_slice_in_dim(block_row, leading_block, NBLK_DEV, 0)
        slots_here = lax.dynamic_slice_in_dim(block_slot, leading_block, NBLK_DEV, 0)
        list_rows = lax.dynamic_slice_in_dim(requests, device * OWNERS, OWNERS, 0)
        is_live = slots_here >= 0
        clamped_slot = jnp.maximum(slots_here, 0)
        owner_index = clamped_slot // CAP
        within = clamped_slot % CAP
        local_index = list_rows[owner_index, within]
        block_upper = (device // SPLIT) * GROUP_BLOCK_ROWS + rows_here
        block_lower = jnp.where(is_live, owner_index * GROUP_BLOCK_ROWS + local_index, 0).astype(jnp.int32)
        pieces = jnp.where(is_live[:, None, None], pieces, jnp.zeros_like(pieces))
        direct = jnp.einsum("kab,kbn->kan", pieces, row_blocks[block_lower])
        mirror = jnp.einsum("kba,kbn->kan", pieces, row_blocks[block_upper])
        summed = summed.at[block_upper].add(direct).at[block_lower].add(mirror)
        return summed, None

    summed, _ = lax.scan(visit_list, jnp.zeros((BLOCKROWS, B, K), jnp.float32), jnp.arange(LISTS, dtype=jnp.int32))
    return summed.reshape(BLOCKROWS * B, K).astype(jnp.bfloat16)


def reference(density_panel, blocks, block_row, block_slot, requests):
    first_product = apply_matrix(density_panel, blocks, block_row, block_slot, requests)
    second_product = apply_matrix(first_product, blocks, block_row, block_slot, requests)
    return (first_product, second_product)
```

```python
import functools

import jax
import jax.numpy as jnp
from jax import lax
from jax.experimental import pallas as pl
from jax.experimental.pallas import tpu as pltpu
from jax.sharding import PartitionSpec as P

B = 64
K = 256
Z, Y, C, X = 8, 4, 2, 4
BF16, F32 = jnp.bfloat16, jnp.float32


def positions(block_row, block_slot):
    z, y, core, t = block_slot // 16, (block_slot // 4) % 4, (block_slot // 2) % 2, block_slot % 2
    place = ((z * C + core) * Y + y) * 16 + t * 8 + block_row
    return jnp.where(block_slot >= 0, place, -1).reshape(1, -1)


def kernel(
    panel, blocks, place, out1, out2,
    matrix, pick, perm, pt, gathered, acc, held, own,
    core_out, core_in, y_out, y_in, z_out, z_in, z_own, x_out, x_in,
    ay_s, ay_r, az_s, az_r, ac_s, ac_r, rc_s, rc_r, ry_s, ry_r, rz_s, rz_r, xr_s, xr_r, xg_s, xg_r,
):
    row, x = lax.axis_index("row"), lax.axis_index("col")
    z, y, k = row // (Y * C), (row // C) % Y, row % C

    def at(zz, yy, kk):
        return (zz * Y + yy) * C + kk

    def copy(src, dst, send, recv, to_row, to_col=None):
        return pltpu.make_async_remote_copy(
            src_ref=src, dst_ref=dst, send_sem=send, recv_sem=recv,
            device_id=(to_row, x if to_col is None else to_col),
            device_id_type=pl.DeviceIdType.MESH,
        )

    barrier = pltpu.get_barrier_semaphore()

    def greet(to_row, to_col):
        pl.semaphore_signal(barrier, inc=1, device_id=(to_row, to_col), device_id_type=pl.DeviceIdType.MESH)

    greet(at(z, y, 1 - k), x)
    for d in range(1, Y):
        greet(at(z, (y + d) % Y, k), x)
    for d in range(1, Z):
        greet(at((z + d) % Z, y, k), x)
    for d in range(1, X):
        greet(row, (x + d) % X)

    r = lax.broadcasted_iota(jnp.int32, (512, 384), 0)
    want = (r // 8) * 16 + r % 8
    at_place = jnp.broadcast_to(place[...], (512, 384))
    pick[:, 0:384] = jnp.where(at_place == want, 1.0, 0.0).astype(BF16)
    pick[:, 384:768] = jnp.where(at_place == want + 8, 1.0, 0.0).astype(BF16)
    j = lax.broadcasted_iota(jnp.int32, (512, 512), 0)
    q = lax.broadcasted_iota(jnp.int32, (512, 512), 1)
    i, a = j % 8, j // 8
    perm[...] = jnp.where(q == ((i % 4) * 2 + i // 4) * 64 + a, 1.0, 0.0).astype(BF16)
    for c in range(X):
        for t in range(2):
            held[0, c, t * 64:(t + 1) * 64, :] = panel[(c + 4 * t) * 64:(c + 4 * t + 1) * 64, :]

    def build(step, carry):
        tile = blocks[:, pl.ds(pl.multiple_of(step * 128, 128), 128)].astype(F32)
        turned = pltpu.roll(tile, 64, 1)
        low = lax.broadcasted_iota(jnp.int32, (384, 128), 1) < 64
        upper = jnp.concatenate([jnp.where(low, tile, 0.0), jnp.where(low, turned, 0.0)], axis=1)
        lower = jnp.concatenate([jnp.where(low, 0.0, turned), jnp.where(low, 0.0, tile)], axis=1)
        both = jnp.concatenate([upper, lower], axis=0).astype(BF16)
        placed = jnp.dot(pick[...], both, preferred_element_type=F32)
        first = placed[:, 0:128].reshape(64, 8, 128)
        second = placed[:, 128:256].reshape(64, 8, 128)
        rows = jnp.concatenate([first, second], axis=1).astype(BF16)
        for chunk in range(64):
            matrix[pl.ds(pl.multiple_of(step * 16, 16), 16), chunk * 128:(chunk + 1) * 128] = rows[chunk]
        return carry

    def ag_y(p, d):
        part = gathered.at[p, z, k, pl.ds(pl.multiple_of(y * 128, 128), 128)]
        return copy(part, part, ay_s.at[p, d - 1], ay_r.at[p, d - 1], at(z, (y + d) % Y, k))

    def ag_z(p, way, s, zo, to):
        unit = gathered.at[p, zo, k]
        return copy(unit, unit, az_s.at[p, way, s - 1], az_r.at[p, way, s - 1], at(to, y, k))

    def ag_core(p, zo):
        unit = gathered.at[p, zo, k]
        return copy(unit, unit, ac_s.at[p, zo], ac_r.at[p, zo], at(z, y, 1 - k))

    def ag_core_arrival(p, zo):
        unit = gathered.at[p, zo, 1 - k]
        return copy(unit, unit, ac_s.at[p, zo], ac_r.at[p, zo], at(z, y, 1 - k))

    def rs_core(p, zo):
        return copy(core_out.at[p, zo], core_in.at[p, zo], rc_s.at[p, zo], rc_r.at[p, zo], at(z, y, 1 - k))

    def rs_y(p, zo, d):
        to = (y + d) % Y
        return copy(y_out.at[p, zo, to], y_in.at[p, zo, d - 1], ry_s.at[p, zo, d - 1], ry_r.at[p, zo, d - 1], at(z, to, k))

    def rs_z(p, zo):
        return copy(z_out.at[p, zo], z_in.at[p, z], rz_s.at[p, zo], rz_r.at[p, z], at(zo, y, k))

    def rs_z_arrival(p, zi):
        return copy(z_out.at[p, zi], z_in.at[p, zi], rz_s.at[p, zi], rz_r.at[p, zi], at(zi, y, k))

    def rs_x(p, d):
        to = (x + d) % X
        return copy(x_out.at[p, to], x_in.at[p, d - 1], xr_s.at[p, d - 1], xr_r.at[p, d - 1], row, to)

    def ag_x(p, d):
        part = held.at[p + 1, x]
        return copy(part, part, xg_s.at[p, d - 1], xg_r.at[p, d - 1], row, (x + d) % X)

    def ag_x_arrival(p, d):
        part = held.at[p + 1, (x + X - d) % X]
        return copy(part, part, xg_s.at[p, d - 1], xg_r.at[p, d - 1], row, (x + d) % X)

    def down_sends(s):
        return (z >= 1) & (z + s - 1 <= 7) & (s <= 4 - k), z + s - 1, z - 1

    def down_gets(s):
        return (z + s <= 7) & (s <= 4 - k), z + s

    def up_sends(s):
        zo = (z + 8 - (s - 1)) % 8
        return (zo >= 5 - k) & (s <= 3 + k), zo, (z + 1) % 8

    def up_gets(s):
        zo = (z + 8 - s) % 8
        return (zo >= 5 - k) & (s <= 3 + k), zo

    def columns(zo, kk):
        return pl.ds(pl.multiple_of((zo * C + kk) * 512, 512), 512)

    def direct(p, zo, kk):
        part = jnp.dot(matrix[:, columns(zo, kk)], gathered[p, zo, kk], preferred_element_type=F32)
        for half in range(2):
            acc[half] += part[:, half * 128:(half + 1) * 128]

    def ag_start(p):
        gathered[p, z, k, pl.ds(pl.multiple_of(y * 128, 128), 128), :] = held[p, x]
        for d in range(1, Y):
            ag_y(p, d).start()

    def ag_pass(p, s):
        cond, zo, to = down_sends(s)

        @pl.when(cond)
        def _():
            ag_z(p, 0, s, zo, to).start()

        cond, zo, to = up_sends(s)

        @pl.when(cond)
        def _():
            ag_z(p, 1, s, zo, to).start()

    def ag_wait(p, s):
        cond, zo = down_gets(s)

        @pl.when(cond)
        def _():
            ag_z(p, 0, s, zo, z).wait_recv()

        cond, zo = up_gets(s)

        @pl.when(cond)
        def _():
            ag_z(p, 1, s, zo, z).wait_recv()

    def ag_use(p, s):
        cond, zo = down_gets(s)

        @pl.when(cond)
        def _():
            ag_core(p, zo).start()
            direct(p, zo, k)

        cond, zo = up_gets(s)

        @pl.when(cond & (zo > z))
        def _():
            ag_core(p, zo).start()
            direct(p, zo, k)

    def ag_first(p):
        for d in range(1, Y):
            ag_y(p, d).wait_recv()
        ag_pass(p, 1)
        ag_core(p, z).start()

    def ag_step(p, s):
        ag_wait(p, s)
        if s < 4:
            ag_pass(p, s + 1)
        ag_use(p, s)

    def others(p):
        def use(zo, carry):
            ag_core_arrival(p, zo).wait_recv()
            direct(p, zo, 1 - k)
            return carry

        lax.fori_loop(z, Z, use, 0)

    def make_pt(p):
        ordered = jnp.dot(perm[...], held[p].reshape(512, 256), preferred_element_type=F32)
        pt[...] = ordered.T.astype(BF16)

    def mirror(zo, kk):
        return jnp.dot(pt[...], matrix[:, columns(zo, kk)], preferred_element_type=F32)

    def rs_a(p):
        def send(step, carry):
            zo = 7 - step
            core_out[p, zo] = mirror(zo, 1 - k).astype(BF16)
            rs_core(p, zo).start()
            return carry

        lax.fori_loop(0, Z - z, send, 0)

    def rs_b(p):
        def send(step, carry):
            zo = 7 - step
            part = mirror(zo, k)
            rs_core(p, zo).wait_recv()
            part = part + core_in[p, zo].astype(F32)
            for to in range(Y):
                piece = part[:, to * 128:(to + 1) * 128]
                own[zo, to] = piece
                y_out[p, zo, to] = piece.astype(BF16)
            for d in range(1, Y):
                rs_y(p, zo, d).start()
            return carry

        lax.fori_loop(0, Z - z, send, 0)

    def rs_c(p, zo):
        @pl.when(zo >= z)
        def _():
            total = own[zo, y]
            for d in range(1, Y):
                rs_y(p, zo, d).wait_recv()
                total = total + y_in[p, zo, d - 1].astype(F32)

            @pl.when(zo > z)
            def _():
                z_out[p, zo] = total.astype(BF16)
                rs_z(p, zo).start()

            @pl.when(zo == z)
            def _():
                z_own[...] = total

    def rs_d(p):
        def add(zi, carry):
            rs_z_arrival(p, zi).wait_recv()
            z_own[...] += z_in[p, zi].astype(F32)
            return carry

        lax.fori_loop(0, z, add, 0)

    def x_start(p):
        for c in range(X):
            for t in range(2):
                for half in range(2):
                    x_out[p, c, t * 64:(t + 1) * 64, half * 128:(half + 1) * 128] = acc[
                        half, pl.ds(c + 4 * t, 64, stride=8), :
                    ]
        for d in range(1, X):
            rs_x(p, d).start()

    def finish(p, out):
        total = x_out[p, x] + z_own[...].T
        for d in range(1, X):
            rs_x(p, d).wait_recv()
            total = total + x_in[p, d - 1]
        held[p + 1, x] = total.astype(BF16)
        for d in range(1, X):
            ag_x(p, d).start()

    def collect(p, out):
        for d in range(1, X):
            ag_x_arrival(p, d).wait_recv()
        for c in range(X):
            for t in range(2):
                out[(c + 4 * t) * 64:(c + 4 * t + 1) * 64, :] = held[p + 1, c, t * 64:(t + 1) * 64, :]

    def product(p, out):
        acc[...] = jnp.zeros_like(acc)
        if p == 0:
            lax.fori_loop(0, 12, build, 0)
            ag_first(p)
            lax.fori_loop(12, 32, build, 0)
        make_pt(p)
        rs_a(p)
        if p == 1:
            ag_first(p)
        rs_b(p)
        direct(p, z, k)
        ag_step(p, 1)
        rs_c(p, 7)
        rs_c(p, 6)
        ag_step(p, 2)
        rs_c(p, 5)
        rs_c(p, 4)
        ag_step(p, 3)
        rs_c(p, 3)
        rs_c(p, 2)
        ag_step(p, 4)
        others(p)
        x_start(p)
        rs_c(p, 1)
        rs_c(p, 0)
        rs_d(p)
        finish(p, out)

    pl.semaphore_wait(barrier, 1 + (Y - 1) + (Z - 1) + (X - 1))
    ag_start(0)
    product(0, out1)
    ag_start(1)
    collect(0, out1)
    product(1, out2)
    collect(1, out2)

    for p in range(2):
        for d in range(1, Y):
            ag_y(p, d).wait_send()
        for d in range(1, X):
            rs_x(p, d).wait_send()
            ag_x(p, d).wait_send()
        for s in range(1, 5):
            cond, zo, to = down_sends(s)

            @pl.when(cond)
            def _():
                ag_z(p, 0, s, zo, to).wait_send()

            cond, zo, to = up_sends(s)

            @pl.when(cond)
            def _():
                ag_z(p, 1, s, zo, to).wait_send()

        def left(zo, carry):
            ag_core(p, zo).wait_send()
            rs_core(p, zo).wait_send()
            for d in range(1, Y):
                rs_y(p, zo, d).wait_send()

            @pl.when(zo > z)
            def _():
                rs_z(p, zo).wait_send()

            return carry

        lax.fori_loop(z, Z, left, 0)


def per_device(density_panel, blocks, block_row, block_slot, requests):
    vmem = pl.BlockSpec(memory_space=pltpu.VMEM)
    dma = pltpu.SemaphoreType.DMA
    shape = jax.ShapeDtypeStruct((512, K), BF16)
    scratch = [
        pltpu.VMEM((512, 8192), BF16),
        pltpu.VMEM((512, 768), BF16),
        pltpu.VMEM((512, 512), BF16),
        pltpu.VMEM((256, 512), BF16),
        pltpu.VMEM((2, Z, C, 512, K), BF16),
        pltpu.VMEM((2, 512, 128), F32),
        pltpu.VMEM((3, X, 128, K), BF16),
        pltpu.VMEM((Z, Y, K, 128), F32),
        pltpu.VMEM((2, Z, K, 512), BF16),
        pltpu.VMEM((2, Z, K, 512), BF16),
        pltpu.VMEM((2, Z, Y, K, 128), BF16),
        pltpu.VMEM((2, Z, Y - 1, K, 128), BF16),
        pltpu.VMEM((2, Z, K, 128), BF16),
        pltpu.VMEM((2, Z, K, 128), BF16),
        pltpu.VMEM((K, 128), F32),
        pltpu.VMEM((2, X, 128, K), F32),
        pltpu.VMEM((2, X - 1, 128, K), F32),
        dma((2, Y - 1)), dma((2, Y - 1)),
        dma((2, 2, 4)), dma((2, 2, 4)),
        dma((2, Z)), dma((2, Z)),
        dma((2, Z)), dma((2, Z)),
        dma((2, Z, Y - 1)), dma((2, Z, Y - 1)),
        dma((2, Z)), dma((2, Z)),
        dma((2, X - 1)), dma((2, X - 1)),
        dma((2, X - 1)), dma((2, X - 1)),
    ]
    return pl.pallas_call(
        kernel,
        out_shape=(shape, shape),
        in_specs=[vmem, vmem, vmem],
        out_specs=(vmem, vmem),
        scratch_shapes=scratch,
        compiler_params=pltpu.CompilerParams(
            collective_id=0, has_side_effects=True, vmem_limit_bytes=60 * 1024 * 1024
        ),
    )(density_panel, blocks, positions(block_row, block_slot))


def solution(mesh):
    in_specs = (
        P("row", None),
        P(("row", "col"), None),
        P(("row", "col")),
        P(("row", "col")),
        P(("row", "col"), None),
    )
    out_specs = (P("row", None), P("row", None))
    return jax.shard_map(
        per_device, mesh=mesh, in_specs=in_specs, out_specs=out_specs, check_vma=False
    )
```

```python
import jax
import jax.numpy as jnp
from jax import lax
from jax.experimental import pallas as pl
from jax.experimental.pallas import tpu as pltpu
from jax.sharding import PartitionSpec as P

B = 64
K = 256
Z, Y, C, X = 8, 4, 2, 4
BF16, F32 = jnp.bfloat16, jnp.float32
RELAY, SUMMED, DIRECT = 0, 1, 2
BUILDS, FIRST_AFTER, STEP_AFTER = 16, 3, (9, 12, 15)


def kernel(
    panel, blocks, block_row, block_slot, out,
    stored, matrix, pick, perm, pt, gathered, acc, held, own,
    core_out, core_in, y_out, y_in, z_out, z_in, z_own, x_out, x_in,
    fetch, ay_s, ay_r, az_s, az_r, ac_s, ac_r, rc_s, rc_r, ry_s, ry_r, rz_s, rz_r, xr_s, xr_r, xg_s, xg_r,
):
    row, x = lax.axis_index("row"), lax.axis_index("col")
    z, y, k = row // (Y * C), (row // C) % Y, row % C
    ahead, behind, across = (y + 1 + 2 * k) % Y, (y + 3 + 2 * k) % Y, (y + 2) % Y

    def at(zz, yy, kk):
        return (zz * Y + yy) * C + kk

    def copy(src, dst, send, recv, to_row, to_col=None):
        return pltpu.make_async_remote_copy(
            src_ref=src, dst_ref=dst, send_sem=send, recv_sem=recv,
            device_id=(to_row, x if to_col is None else to_col),
            device_id_type=pl.DeviceIdType.MESH,
        )

    def load(part):
        lanes = pl.ds(pl.multiple_of(part * 1024, 1024), 1024)
        return pltpu.make_async_copy(blocks.at[:, lanes], stored.at[:, lanes], fetch.at[part])

    for part in range(4):
        load(part).start()
    barrier = pltpu.get_barrier_semaphore()

    def greet(to_row, to_col):
        pl.semaphore_signal(barrier, inc=1, device_id=(to_row, to_col), device_id_type=pl.DeviceIdType.MESH)

    greet(at(z, y, 1 - k), x)
    for d in range(1, Y):
        greet(at(z, (y + d) % Y, k), x)
    for d in range(1, Z):
        greet(at((z + d) % Z, y, k), x)
    for d in range(1, X):
        greet(row, (x + d) % X)

    for h in range(2):
        for c in range(X):
            for t in range(2):
                held[0, h, c, t * 64:(t + 1) * 64, :] = panel[
                    (c + 4 * t) * 64:(c + 4 * t + 1) * 64, h * 128:(h + 1) * 128
                ]

    def set_up():
        slot = block_slot[...]
        chunk_of = ((slot // 16) * C + (slot // 2) % 2) * Y + (slot // 4) % 4
        place = jnp.where(slot >= 0, chunk_of * 16 + (slot % 2) * 8 + block_row[...], -1)
        r = lax.broadcasted_iota(jnp.int32, (512, 384), 0)
        want = (r // 8) * 16 + r % 8
        at_place = jnp.broadcast_to(place, (512, 384))
        pick[:, 0:384] = jnp.where(at_place == want, 1.0, 0.0).astype(BF16)
        pick[:, 384:768] = jnp.where(at_place == want + 8, 1.0, 0.0).astype(BF16)
        j = lax.broadcasted_iota(jnp.int32, (512, 512), 0)
        q = lax.broadcasted_iota(jnp.int32, (512, 512), 1)
        i, a = j % 8, j // 8
        perm[...] = jnp.where(q == ((i % 4) * 2 + i // 4) * 64 + a, 1.0, 0.0).astype(BF16)

    def build(step):
        tile = stored[:, pl.ds(pl.multiple_of(step * 128, 128), 128)].astype(F32)
        turned = pltpu.roll(tile, 64, 1)
        low = lax.broadcasted_iota(jnp.int32, (384, 128), 1) < 64
        upper = jnp.concatenate([jnp.where(low, tile, 0.0), jnp.where(low, turned, 0.0)], axis=1)
        lower = jnp.concatenate([jnp.where(low, 0.0, turned), jnp.where(low, 0.0, tile)], axis=1)
        both = jnp.concatenate([upper, lower], axis=0).astype(BF16)
        placed = jnp.dot(pick[...], both, preferred_element_type=F32)
        first = placed[:, 0:128].reshape(64, 8, 128)
        second = placed[:, 128:256].reshape(64, 8, 128)
        rows = jnp.concatenate([first, second], axis=1).astype(BF16)
        for chunk in range(64):
            matrix[pl.ds(pl.multiple_of(step * 16, 16), 16), chunk * 128:(chunk + 1) * 128] = rows[chunk]

    def ag_y(p, h, d):
        part = gathered.at[p, h, z, k, pl.ds(pl.multiple_of(y * 128, 128), 128)]
        return copy(part, part, ay_s.at[p, h, d - 1], ay_r.at[p, h, d - 1], at(z, (y + d) % Y, k))

    def ag_z(p, h, way, s, zo, to):
        unit = gathered.at[p, h, zo, k]
        return copy(unit, unit, az_s.at[p, h, way, s - 1], az_r.at[p, h, way, s - 1], at(to, y, k))

    def ag_core(p, h, zo, kk):
        unit = gathered.at[p, h, zo, kk]
        return copy(unit, unit, ac_s.at[p, h, zo], ac_r.at[p, h, zo], at(z, y, 1 - k))

    def rs_core(p, zo):
        return copy(core_out.at[p, zo], core_in.at[p, zo], rc_s.at[p, zo], rc_r.at[p, zo], at(z, y, 1 - k))

    def rs_y(p, zo, what):
        to = behind if what == DIRECT else ahead
        return copy(y_out.at[p, zo, what], y_in.at[p, zo, what], ry_s.at[p, zo, what], ry_r.at[p, zo, what], at(z, to, k))

    def rs_z(p, zo, frm):
        return copy(z_out.at[p, zo], z_in.at[p, frm], rz_s.at[p, zo], rz_r.at[p, frm], at(zo, y, k))

    def rs_x(p, h, d):
        to = (x + d) % X
        return copy(x_out.at[p, h, to], x_in.at[p, h, d - 1], xr_s.at[p, h, d - 1], xr_r.at[p, h, d - 1], row, to)

    def ag_x(p, h, d, frm):
        part = held.at[p + 1, h, frm]
        return copy(part, part, xg_s.at[p, h, d - 1], xg_r.at[p, h, d - 1], row, (x + d) % X)

    def ring_send(way, s):
        down = (z >= 1) & (z + s - 1 <= 7) & (s <= 4 - k)
        up_zo = (z + 9 - s) % 8
        up = (up_zo >= 5 - k) & (s <= 3 + k)
        if way == 0:
            return down, z + s - 1, z - 1
        return up, up_zo, (z + 1) % 8

    def ring_get(way, s, kk):
        if way == 0:
            return (z + s <= 7) & (s <= 4 - kk), z + s
        zo = (z + 8 - s) % 8
        return (zo >= 5 - kk) & (s <= 3 + kk), zo

    def columns(zo, kk):
        return pl.ds(pl.multiple_of((zo * C + kk) * 512, 512), 512)

    def direct_both(p, zo, kk):
        wide = jnp.concatenate([gathered[p, 0, zo, kk], gathered[p, 1, zo, kk]], axis=1)
        part = jnp.dot(matrix[:, columns(zo, kk)], wide, preferred_element_type=F32)
        for h in range(2):
            acc[h] += part[:, h * 128:(h + 1) * 128]

    def direct_half(p, h, zo, kk):
        acc[h] += jnp.dot(matrix[:, columns(zo, kk)], gathered[p, h, zo, kk], preferred_element_type=F32)

    def ag_start(p, h):
        gathered[p, h, z, k, pl.ds(pl.multiple_of(y * 128, 128), 128), :] = held[p, h, x]
        for d in range(1, Y):
            ag_y(p, h, d).start()

    def ag_pass(p, h, s):
        for way in range(2):
            cond, zo, to = ring_send(way, s)

            @pl.when(cond)
            def _():
                ag_z(p, h, way, s, zo, to).start()

    def ag_first(p, h):
        for d in range(1, Y):
            ag_y(p, h, d).wait_recv()
        ag_pass(p, h, 1)
        ag_core(p, h, z, k).start()

    def ag_own(p):
        acc[...] = jnp.zeros_like(acc)

        def use(kk, carry):
            @pl.when(kk != k)
            def _():
                for h in range(2):
                    ag_core(p, h, z, kk).wait_recv()

            direct_both(p, z, kk)
            return carry

        lax.fori_loop(0, C, use, 0)

    def ag_step(p, e):
        s, h = 1 + e // 2, e % 2
        for way in range(2):
            cond, zo = ring_get(way, s, k)

            @pl.when(cond)
            def _():
                ag_z(p, h, way, s, zo, z).wait_recv()

        @pl.when(s < 4)
        def _():
            ag_pass(p, h, s + 1)

        for way in range(2):
            cond, zo = ring_get(way, s, k)

            @pl.when(cond & (zo > z))
            def _():
                ag_core(p, h, zo, k).start()

    def ag_use(p, e, mine):
        s, h = 1 + e // 2, e % 2

        def use(way, carry):
            kk = k if mine else 1 - k
            down, zd = ring_get(0, s, kk)
            up, zu = ring_get(1, s, kk)
            zo = jnp.where(way == 0, zd, zu)
            cond = ((way == 0) & down | (way == 1) & up) & (zo > z)

            @pl.when(cond)
            def _():
                if not mine:
                    ag_core(p, h, zo, kk).wait_recv()

                @pl.when(s == 4)
                def _():
                    direct_half(p, h, zo, kk)

                @pl.when((s < 4) & (h == 1))
                def _():
                    direct_both(p, zo, kk)

            return carry

        lax.fori_loop(0, 2, use, 0)

    def make_pt(p):
        for h in range(2):
            ordered = jnp.dot(perm[...], held[p, h].reshape(512, 128), preferred_element_type=F32)
            pt[h * 128:(h + 1) * 128, :] = ordered.T.astype(BF16)

    def mirror(zo, kk):
        return jnp.dot(pt[...], matrix[:, columns(zo, kk)], preferred_element_type=F32)

    def rs_a(p, zo):
        core_out[p, zo] = mirror(zo, 1 - k).astype(BF16)
        rs_core(p, zo).start()

    def rs_b1(p, zo):
        part = mirror(zo, k)
        rs_core(p, zo).wait_recv()
        part = part + core_in[p, zo].astype(F32)
        for to in range(Y):
            own[zo, to] = part[:, to * 128:(to + 1) * 128]
        y_out[p, zo, RELAY] = own[zo, across].astype(BF16)
        rs_y(p, zo, RELAY).start()
        y_out[p, zo, DIRECT] = own[zo, behind].astype(BF16)
        rs_y(p, zo, DIRECT).start()

    def rs_b2(p, zo):
        rs_y(p, zo, RELAY).wait_recv()
        y_out[p, zo, SUMMED] = (own[zo, ahead] + y_in[p, zo, RELAY].astype(F32)).astype(BF16)
        rs_y(p, zo, SUMMED).start()

    def rs_c(p, zo):
        rs_y(p, zo, DIRECT).wait_recv()
        rs_y(p, zo, SUMMED).wait_recv()
        total = own[zo, y] + y_in[p, zo, DIRECT].astype(F32) + y_in[p, zo, SUMMED].astype(F32)

        @pl.when(zo > z)
        def _():
            z_out[p, zo] = total.astype(BF16)

            @pl.when(jnp.logical_not(waits(zo)))
            def _():
                rs_z(p, zo, z).start()

        @pl.when(zo == z)
        def _():
            z_own[...] = total

    def waits(zo):
        return (z >= 1) & (zo - z >= 4)

    def rs_late(p):
        for zo in range(5, Z):
            @pl.when(waits(zo))
            def _():
                rs_z(p, zo, z).start()

    def rs_d(p):
        def add(zi, carry):
            rs_z(p, zi, zi).wait_recv()
            z_own[...] += z_in[p, zi].astype(F32)
            return carry

        lax.fori_loop(0, z, add, 0)

    def x_start(p, h):
        for c in range(X):
            for t in range(2):
                x_out[p, h, c, t * 64:(t + 1) * 64, :] = acc[h, pl.ds(c + 4 * t, 64, stride=8), :]
        for d in range(1, X):
            rs_x(p, h, d).start()

    def finish(p, h):
        total = x_out[p, h, x] + z_own[h * 128:(h + 1) * 128, :].T
        for d in range(1, X):
            rs_x(p, h, d).wait_recv()
            total = total + x_in[p, h, d - 1]
        held[p + 1, h, x] = total.astype(BF16)
        for d in range(1, X):
            ag_x(p, h, d, x).start()

    def collect(p):
        for h in range(2):
            for d in range(1, X):
                ag_x(p, h, d, (x + X - d) % X).wait_recv()
        out[p] = held[p + 1]

    def product(p, carry):
        for h in range(2):
            ag_start(p, h)

        @pl.when(p == 0)
        def _():
            set_up()

            def build_some(part, carry):
                @pl.when(part % (BUILDS // 4) == 0)
                def _():
                    load(part // (BUILDS // 4)).wait()

                for n in range(32 // BUILDS):
                    build(part * (32 // BUILDS) + n)

                @pl.when(part == FIRST_AFTER)
                def _():
                    for h in range(2):
                        ag_first(p, h)

                for e, after in enumerate(STEP_AFTER):
                    @pl.when(part == after)
                    def _():
                        ag_step(p, e)

                return carry

            lax.fori_loop(0, BUILDS, build_some, 0)

        @pl.when(p == 1)
        def _():
            for h in range(2):
                ag_first(p, h)
            collect(0)

        make_pt(p)
        lead = jnp.where(p == 0, -3, 0)

        def turn(step, carry):
            n = step - 6

            def stage(first, body, count=8, skip=0):
                @pl.when((n >= first + skip) & (n < first + count))
                def _():
                    body(n - first)

            def stage_zo(first, body):
                zo = 7 - (n - first)

                @pl.when((n >= first) & (zo >= z))
                def _():
                    body(p, zo)

            stage_zo(-3, rs_a)
            stage_zo(-2, rs_b1)
            stage(lead, lambda e: ag_step(p, e), 8, jnp.where(p == 0, len(STEP_AFTER), 0))
            stage_zo(0, rs_b2)
            stage_zo(3, rs_c)
            stage(jnp.where(p == 0, -6, -1), lambda e: ag_own(p), 1)
            stage(lead, lambda e: ag_use(p, e, True))
            stage(lead + 1, lambda e: ag_use(p, e, False))
            stage(lead + 7, lambda e: x_start(p, e), 2)
            stage(jnp.where(p == 0, 6, 8), lambda e: rs_late(p), 1)
            return carry

        lax.fori_loop(0, 17, turn, 0)
        rs_d(p)
        for h in range(2):
            finish(p, h)
        return carry

    pl.semaphore_wait(barrier, 1 + (Y - 1) + (Z - 1) + (X - 1))
    lax.fori_loop(0, 2, product, 0)
    collect(1)

    def left(p, carry):
        for h in range(2):
            for d in range(1, Y):
                ag_y(p, h, d).wait_send()
            for d in range(1, X):
                rs_x(p, h, d).wait_send()
                ag_x(p, h, d, x).wait_send()
            for way in range(2):
                for s in range(1, 5):
                    cond, zo, to = ring_send(way, s)

                    @pl.when(cond)
                    def _():
                        ag_z(p, h, way, s, zo, to).wait_send()

        def left_zo(zo, carry):
            for h in range(2):
                ag_core(p, h, zo, k).wait_send()
            rs_core(p, zo).wait_send()
            for what in (RELAY, SUMMED, DIRECT):
                rs_y(p, zo, what).wait_send()

            @pl.when(zo > z)
            def _():
                rs_z(p, zo, z).wait_send()

            return carry

        lax.fori_loop(z, Z, left_zo, 0)
        return carry

    lax.fori_loop(0, 2, left, 0)


def lay_out(held, out1, out2):
    for p, out in enumerate((out1, out2)):
        for h in range(2):
            for c in range(X):
                for t in range(2):
                    out[(c + 4 * t) * 64:(c + 4 * t + 1) * 64, h * 128:(h + 1) * 128] = held[
                        p, h, c, t * 64:(t + 1) * 64, :
                    ]


def per_device(density_panel, blocks, block_row, block_slot, requests):
    vmem = pl.BlockSpec(memory_space=pltpu.VMEM)
    dma = pltpu.SemaphoreType.DMA
    shape = jax.ShapeDtypeStruct((512, K), BF16)

    def pair(*dims):
        return [dma(dims), dma(dims)]

    scratch = [
        pltpu.VMEM((384, 4096), BF16),
        pltpu.VMEM((512, 8192), BF16),
        pltpu.VMEM((512, 768), BF16),
        pltpu.VMEM((512, 512), BF16),
        pltpu.VMEM((256, 512), BF16),
        pltpu.VMEM((2, 2, Z, C, 512, 128), BF16),
        pltpu.VMEM((2, 512, 128), F32),
        pltpu.VMEM((3, 2, X, 128, 128), BF16),
        pltpu.VMEM((Z, Y, K, 128), F32),
        pltpu.VMEM((2, Z, K, 512), BF16),
        pltpu.VMEM((2, Z, K, 512), BF16),
        pltpu.VMEM((2, Z, 3, K, 128), BF16),
        pltpu.VMEM((2, Z, 3, K, 128), BF16),
        pltpu.VMEM((2, Z, K, 128), BF16),
        pltpu.VMEM((2, Z, K, 128), BF16),
        pltpu.VMEM((K, 128), F32),
        pltpu.VMEM((2, 2, X, 128, 128), F32),
        pltpu.VMEM((2, 2, X - 1, 128, 128), F32),
        dma((4,)),
        *pair(2, 2, Y - 1),
        *pair(2, 2, 2, 4),
        *pair(2, 2, Z),
        *pair(2, Z),
        *pair(2, Z, 3),
        *pair(2, Z),
        *pair(2, 2, X - 1),
        *pair(2, 2, X - 1),
    ]
    held = pl.pallas_call(
        kernel,
        out_shape=jax.ShapeDtypeStruct((2, 2, X, 128, 128), BF16),
        in_specs=[vmem, pl.BlockSpec(memory_space=pl.ANY), vmem, vmem],
        out_specs=vmem,
        scratch_shapes=scratch,
        compiler_params=pltpu.CompilerParams(
            collective_id=0, has_side_effects=True, vmem_limit_bytes=60 * 1024 * 1024
        ),
    )(density_panel, blocks, block_row, block_slot)
    return pl.pallas_call(
        lay_out, out_shape=(shape, shape), in_specs=[vmem], out_specs=(vmem, vmem)
    )(held)


def solution(mesh):
    in_specs = (
        P("row", None),
        P(("row", "col"), None),
        P(("row", "col")),
        P(("row", "col")),
        P(("row", "col"), None),
    )
    out_specs = (P("row", None), P("row", None))
    return jax.shard_map(
        per_device, mesh=mesh, in_specs=in_specs, out_specs=out_specs, check_vma=False
    )
```

```python
import jax
import jax.numpy as jnp
from jax import lax
from jax.experimental import pallas as pl
from jax.experimental.pallas import tpu as pltpu
from jax.sharding import PartitionSpec as P

B = 64
K = 256
Z, Y, C, X = 8, 4, 2, 4
BF16, F32 = jnp.bfloat16, jnp.float32
RELAY, SUMMED, DIRECT = 0, 1, 2
FIRST_AFTER = 3


def kernel(
    panel, blocks, block_row, block_slot, out,
    stored, matrix, pick, perm, pt, gathered, acc, held, own,
    core_out, core_in, y_out, y_in, z_out, z_in, z_own, x_out, x_in,
    fetch, ay_s, ay_r, az_s, az_r, af_s, af_r, ag_s, ag_r, ac_s, ac_r, rc_s, rc_r, ry_s, ry_r, rz_s, rz_r, xr_s, xr_r, xg_s, xg_r,
):
    row, x = lax.axis_index("row"), lax.axis_index("col")
    z, y, k = row // (Y * C), (row // C) % Y, row % C
    ahead, behind, across = (y + 1 + 2 * k) % Y, (y + 3 + 2 * k) % Y, (y + 2) % Y

    def at(zz, yy, kk):
        return (zz * Y + yy) * C + kk

    def copy(src, dst, send, recv, to_row, to_col=None):
        return pltpu.make_async_remote_copy(
            src_ref=src, dst_ref=dst, send_sem=send, recv_sem=recv,
            device_id=(to_row, x if to_col is None else to_col),
            device_id_type=pl.DeviceIdType.MESH,
        )

    def load(part):
        lanes = pl.ds(pl.multiple_of(part * 1024, 1024), 1024)
        return pltpu.make_async_copy(blocks.at[:, lanes], stored.at[:, lanes], fetch.at[part])

    for part in range(4):
        load(part).start()
    barrier = pltpu.get_barrier_semaphore()

    def greet(to_row, to_col):
        pl.semaphore_signal(barrier, inc=1, device_id=(to_row, to_col), device_id_type=pl.DeviceIdType.MESH)

    greet(at(z, y, 1 - k), x)
    for d in range(1, Y):
        greet(at(z, (y + d) % Y, k), x)
    for d in range(1, Z):
        greet(at((z + d) % Z, y, k), x)
    for d in range(1, X):
        greet(row, (x + d) % X)

    for h in range(2):
        for c in range(X):
            for t in range(2):
                held[0, h, c, t * 64:(t + 1) * 64, :] = panel[
                    (c + 4 * t) * 64:(c + 4 * t + 1) * 64, h * 128:(h + 1) * 128
                ]

    def set_up():
        slot = block_slot[...]
        chunk_of = ((slot // 16) * C + (slot // 2) % 2) * Y + (slot // 4) % 4
        place = jnp.where(slot >= 0, chunk_of * 16 + (slot % 2) * 8 + block_row[...], -1)
        r = lax.broadcasted_iota(jnp.int32, (512, 384), 0)
        want = (r // 8) * 16 + r % 8
        at_place = jnp.broadcast_to(place, (512, 384))
        pick[:, 0:384] = jnp.where(at_place == want, 1.0, 0.0).astype(BF16)
        pick[:, 384:768] = jnp.where(at_place == want + 8, 1.0, 0.0).astype(BF16)
        j = lax.broadcasted_iota(jnp.int32, (512, 512), 0)
        q = lax.broadcasted_iota(jnp.int32, (512, 512), 1)
        i, a = j % 8, j // 8
        perm[...] = jnp.where(q == ((i % 4) * 2 + i // 4) * 64 + a, 1.0, 0.0).astype(BF16)

    def build(step, half):
        tile = stored[:, pl.ds(pl.multiple_of(step * 128, 128), 128)].astype(F32)
        turned = pltpu.roll(tile, 64, 1)
        low = lax.broadcasted_iota(jnp.int32, (384, 128), 1) < 64
        upper = jnp.concatenate([jnp.where(low, tile, 0.0), jnp.where(low, turned, 0.0)], axis=1)
        lower = jnp.concatenate([jnp.where(low, 0.0, turned), jnp.where(low, 0.0, tile)], axis=1)
        both = jnp.concatenate([upper, lower], axis=0).astype(BF16)
        placed = jnp.dot(pick[half * 256:(half + 1) * 256, :], both, preferred_element_type=F32)
        first = placed[:, 0:128].reshape(32, 8, 128)
        second = placed[:, 128:256].reshape(32, 8, 128)
        rows = jnp.concatenate([first, second], axis=1).astype(BF16)
        for chunk in range(32):
            start = (half * 32 + chunk) * 128
            matrix[pl.ds(pl.multiple_of(step * 16, 16), 16), start:start + 128] = rows[chunk]

    def ag_y(p, h, d):
        part = gathered.at[p, h, z, k, pl.ds(pl.multiple_of(y * 128, 128), 128)]
        return copy(part, part, ay_s.at[p, h, d - 1], ay_r.at[p, h, d - 1], at(z, (y + d) % Y, k))

    def ag_z(p, h, way, s, zo, to):
        unit = gathered.at[p, h, zo, k]
        return copy(unit, unit, az_s.at[p, h, way, s - 1], az_r.at[p, h, way, s - 1], at(to, y, k))

    def ag_core(p, h, zo, kk):
        unit = gathered.at[p, h, zo, kk]
        return copy(unit, unit, ac_s.at[p, h, zo], ac_r.at[p, h, zo], at(z, y, 1 - k))

    def rs_core(p, zo):
        return copy(core_out.at[p, zo], core_in.at[p, zo], rc_s.at[p, zo], rc_r.at[p, zo], at(z, y, 1 - k))

    def rs_y(p, zo, what):
        to = behind if what == DIRECT else ahead
        return copy(y_out.at[p, zo, what], y_in.at[p, zo, what], ry_s.at[p, zo, what], ry_r.at[p, zo, what], at(z, to, k))

    def rs_z(p, zo, frm):
        return copy(z_out.at[p, zo], z_in.at[p, frm], rz_s.at[p, zo], rz_r.at[p, frm], at(zo, y, k))

    def rs_x(p, h, d):
        to = (x + d) % X
        return copy(x_out.at[p, h, to], x_in.at[p, h, d - 1], xr_s.at[p, h, d - 1], xr_r.at[p, h, d - 1], row, to)

    def ag_x(p, h, d, frm):
        part = held.at[p + 1, h, frm]
        return copy(part, part, xg_s.at[p, h, d - 1], xg_r.at[p, h, d - 1], row, (x + d) % X)

    def ag_far(p, h, zo, to):
        part = gathered.at[p, h, zo, k, pl.ds(pl.multiple_of(y * 128, 128), 128)]
        return copy(part, part, af_s.at[p, h], af_r.at[p, h], at(to, y, k))

    def ag_far_y(p, h, d):
        part = gathered.at[p, h, z + 4, k, pl.ds(pl.multiple_of(y * 128, 128), 128)]
        return copy(part, part, ag_s.at[p, h, d - 1], ag_r.at[p, h, d - 1], at(z, (y + d) % Y, k))

    def ring_send(way, s):
        down = (z >= 1) & (z + s - 1 <= 7) & (s <= 3)
        up_zo = (z + 9 - s) % 8
        up = (up_zo >= 5) & (s <= 3)
        if way == 0:
            return down, z + s - 1, z - 1
        return up, up_zo, (z + 1) % 8

    def ring_get(way, s):
        if way == 0:
            return (z + s <= 7) & (s <= 3), z + s
        zo = (z + 8 - s) % 8
        return (zo >= 5) & (s <= 3), zo

    def columns(zo, kk):
        return pl.ds(pl.multiple_of((zo * C + kk) * 512, 512), 512)

    def direct_both(p, zo, kk):
        wide = jnp.concatenate([gathered[p, 0, zo, kk], gathered[p, 1, zo, kk]], axis=1)
        part = jnp.dot(matrix[:, columns(zo, kk)], wide, preferred_element_type=F32)
        for h in range(2):
            acc[h] += part[:, h * 128:(h + 1) * 128]

    def direct_half(p, h, zo, kk):
        acc[h] += jnp.dot(matrix[:, columns(zo, kk)], gathered[p, h, zo, kk], preferred_element_type=F32)

    def ag_start(p, h):
        gathered[p, h, z, k, pl.ds(pl.multiple_of(y * 128, 128), 128), :] = held[p, h, x]
        for d in range(1, Y):
            ag_y(p, h, d).start()

        @pl.when(z >= 4)
        def _():
            ag_far(p, h, z, z - 4).start()

    def ag_pass(p, h, s):
        for way in range(2):
            cond, zo, to = ring_send(way, s)

            @pl.when(cond)
            def _():
                ag_z(p, h, way, s, zo, to).start()

    def ag_first(p, h):
        for d in range(1, Y):
            ag_y(p, h, d).wait_recv()
        ag_pass(p, h, 1)
        ag_core(p, h, z, k).start()

    def far_pass(p):
        @pl.when(z < 4)
        def _():
            for h in range(2):
                ag_far(p, h, z + 4, z).wait_recv()
                for d in range(1, Y):
                    ag_far_y(p, h, d).start()

    def far_core(p):
        @pl.when(z < 4)
        def _():
            for h in range(2):
                for d in range(1, Y):
                    ag_far_y(p, h, d).wait_recv()
                ag_core(p, h, z + 4, k).start()

    def far_use(p):
        @pl.when(z < 4)
        def _():
            direct_both(p, z + 4, k)
            for h in range(2):
                ag_core(p, h, z + 4, 1 - k).wait_recv()
            direct_both(p, z + 4, 1 - k)

    def ag_own(p):
        acc[...] = jnp.zeros_like(acc)

        def use(kk, carry):
            @pl.when(kk != k)
            def _():
                for h in range(2):
                    ag_core(p, h, z, kk).wait_recv()

            direct_both(p, z, kk)
            return carry

        lax.fori_loop(0, C, use, 0)

    def ag_step(p, e):
        s, h = 1 + e // 2, e % 2
        for way in range(2):
            cond, zo = ring_get(way, s)

            @pl.when(cond)
            def _():
                ag_z(p, h, way, s, zo, z).wait_recv()

        @pl.when(s < 3)
        def _():
            ag_pass(p, h, s + 1)

        for way in range(2):
            cond, zo = ring_get(way, s)

            @pl.when(cond & (zo > z))
            def _():
                ag_core(p, h, zo, k).start()

    def ag_use(p, e, mine):
        s, h = 1 + e // 2, e % 2

        def use(way, carry):
            kk = k if mine else 1 - k
            down, zd = ring_get(0, s)
            up, zu = ring_get(1, s)
            zo = jnp.where(way == 0, zd, zu)
            cond = ((way == 0) & down | (way == 1) & up) & (zo > z)

            @pl.when(cond)
            def _():
                if not mine:
                    ag_core(p, h, zo, kk).wait_recv()

                @pl.when(s == 3)
                def _():
                    direct_half(p, h, zo, kk)

                @pl.when((s < 3) & (h == 1))
                def _():
                    direct_both(p, zo, kk)

            return carry

        lax.fori_loop(0, 2, use, 0)

    def make_pt(p):
        for h in range(2):
            ordered = jnp.dot(perm[...], held[p, h].reshape(512, 128), preferred_element_type=F32)
            pt[h * 128:(h + 1) * 128, :] = ordered.T.astype(BF16)

    def mirror(zo, kk):
        return jnp.dot(pt[...], matrix[:, columns(zo, kk)], preferred_element_type=F32)

    def rs_a(p, zo):
        core_out[p, zo] = mirror(zo, 1 - k).astype(BF16)
        rs_core(p, zo).start()

    def rs_b1(p, zo):
        part = mirror(zo, k)
        rs_core(p, zo).wait_recv()
        part = part + core_in[p, zo].astype(F32)
        for to in range(Y):
            own[zo, to] = part[:, to * 128:(to + 1) * 128]
        y_out[p, zo, RELAY] = own[zo, across].astype(BF16)
        rs_y(p, zo, RELAY).start()
        y_out[p, zo, DIRECT] = own[zo, behind].astype(BF16)
        rs_y(p, zo, DIRECT).start()

    def rs_b2(p, zo):
        rs_y(p, zo, RELAY).wait_recv()
        y_out[p, zo, SUMMED] = (own[zo, ahead] + y_in[p, zo, RELAY].astype(F32)).astype(BF16)
        rs_y(p, zo, SUMMED).start()

    def rs_c(p, zo):
        rs_y(p, zo, DIRECT).wait_recv()
        rs_y(p, zo, SUMMED).wait_recv()
        total = own[zo, y] + y_in[p, zo, DIRECT].astype(F32) + y_in[p, zo, SUMMED].astype(F32)

        @pl.when(zo > z)
        def _():
            z_out[p, zo] = total.astype(BF16)

            @pl.when(jnp.logical_not(waits(zo)))
            def _():
                rs_z(p, zo, z).start()

        @pl.when(zo == z)
        def _():
            z_own[...] = total

    def waits(zo):
        return (z >= 1) & (zo - z >= 4)

    def rs_late(p):
        for zo in range(5, Z):
            @pl.when(waits(zo))
            def _():
                rs_z(p, zo, z).start()

    def rs_d(p):
        def add(zi, carry):
            rs_z(p, zi, zi).wait_recv()
            z_own[...] += z_in[p, zi].astype(F32)
            return carry

        lax.fori_loop(0, z, add, 0)

    def x_start(p, h):
        for c in range(X):
            for t in range(2):
                x_out[p, h, c, t * 64:(t + 1) * 64, :] = acc[h, pl.ds(c + 4 * t, 64, stride=8), :]
        for d in range(1, X):
            rs_x(p, h, d).start()

    def finish(p, h):
        total = x_out[p, h, x] + z_own[h * 128:(h + 1) * 128, :].T
        for d in range(1, X):
            rs_x(p, h, d).wait_recv()
            total = total + x_in[p, h, d - 1]
        held[p + 1, h, x] = total.astype(BF16)
        for d in range(1, X):
            ag_x(p, h, d, x).start()

    def collect(p):
        for h in range(2):
            for d in range(1, X):
                ag_x(p, h, d, (x + X - d) % X).wait_recv()
        out[p] = held[p + 1]

    def build_rest(e):
        def build_some(part, carry):
            for n in range(4):
                build(part * 4 + n, 0)
            return carry

        @pl.when(z < 4)
        def _():
            lax.fori_loop(e * 4, e * 4 + 4, build_some, 0)

    def product(p, carry):
        for h in range(2):
            ag_start(p, h)

        @pl.when(p == 0)
        def _():
            set_up()

            def build_some(part, carry):
                @pl.when(part % 2 == 0)
                def _():
                    load(part // 2).wait()

                for n in range(4):
                    build(part * 4 + n, 1)

                @pl.when(part == FIRST_AFTER)
                def _():
                    for h in range(2):
                        ag_first(p, h)

                return carry

            lax.fori_loop(0, 8, build_some, 0)

        @pl.when(p == 1)
        def _():
            for h in range(2):
                ag_first(p, h)
            collect(0)

        make_pt(p)
        lead = jnp.where(p == 0, -2, 0)
        use = 1 - p

        def turn(step, carry):
            n = step - 3

            def stage(first, body, count):
                @pl.when((n >= first) & (n < first + count))
                def _():
                    body(n - first)

            def stage_zo(first, body):
                zo = 7 - (n - first)

                @pl.when((n >= first) & (zo >= z))
                def _():
                    body(p, zo)

            stage_zo(-3, rs_a)
            stage_zo(-2, rs_b1)
            stage(lead, lambda e: ag_step(p, e), 6)
            stage(jnp.where(p == 0, -3, -2), lambda e: far_pass(p), 1)
            stage_zo(0, rs_b2)
            stage_zo(3, rs_c)
            stage(jnp.where(p == 0, -1, 1), lambda e: far_core(p), 1)
            stage(jnp.where(p == 0, -1, 99), build_rest, 2)
            stage(1 - 2 * p, lambda e: ag_own(p), 1)
            stage(2, lambda e: far_use(p), 1)
            stage(use, lambda e: ag_use(p, e, True), 6)
            stage(use + 1, lambda e: ag_use(p, e, False), 6)
            stage(use + 5, lambda e: x_start(p, e), 2)
            stage(jnp.where(p == 0, 6, 7), lambda e: rs_late(p), 1)
            return carry

        lax.fori_loop(0, 14, turn, 0)
        rs_d(p)
        for h in range(2):
            finish(p, h)
        return carry

    pl.semaphore_wait(barrier, 1 + (Y - 1) + (Z - 1) + (X - 1))
    lax.fori_loop(0, 2, product, 0)

    def left(p, carry):
        for h in range(2):
            for d in range(1, Y):
                ag_y(p, h, d).wait_send()

            @pl.when(z >= 4)
            def _():
                ag_far(p, h, z, z - 4).wait_send()

            @pl.when(z < 4)
            def _():
                for d in range(1, Y):
                    ag_far_y(p, h, d).wait_send()

            for d in range(1, X):
                rs_x(p, h, d).wait_send()
                ag_x(p, h, d, x).wait_send()
            for way in range(2):
                for s in range(1, 4):
                    cond, zo, to = ring_send(way, s)

                    @pl.when(cond)
                    def _():
                        ag_z(p, h, way, s, zo, to).wait_send()

        def left_zo(zo, carry):
            for h in range(2):
                ag_core(p, h, zo, k).wait_send()
            rs_core(p, zo).wait_send()
            for what in (RELAY, SUMMED, DIRECT):
                rs_y(p, zo, what).wait_send()

            @pl.when(zo > z)
            def _():
                rs_z(p, zo, z).wait_send()

            return carry

        lax.fori_loop(z, Z, left_zo, 0)
        return carry

    lax.fori_loop(0, 2, left, 0)
    collect(1)


def lay_out(held, out1, out2):
    for p, out in enumerate((out1, out2)):
        for h in range(2):
            for c in range(X):
                for t in range(2):
                    out[(c + 4 * t) * 64:(c + 4 * t + 1) * 64, h * 128:(h + 1) * 128] = held[
                        p, h, c, t * 64:(t + 1) * 64, :
                    ]


def per_device(density_panel, blocks, block_row, block_slot, requests):
    vmem = pl.BlockSpec(memory_space=pltpu.VMEM)
    dma = pltpu.SemaphoreType.DMA
    shape = jax.ShapeDtypeStruct((512, K), BF16)

    def pair(*dims):
        return [dma(dims), dma(dims)]

    scratch = [
        pltpu.VMEM((384, 4096), BF16),
        pltpu.VMEM((512, 8192), BF16),
        pltpu.VMEM((512, 768), BF16),
        pltpu.VMEM((512, 512), BF16),
        pltpu.VMEM((256, 512), BF16),
        pltpu.VMEM((2, 2, Z, C, 512, 128), BF16),
        pltpu.VMEM((2, 512, 128), F32),
        pltpu.VMEM((3, 2, X, 128, 128), BF16),
        pltpu.VMEM((Z, Y, K, 128), F32),
        pltpu.VMEM((2, Z, K, 512), BF16),
        pltpu.VMEM((2, Z, K, 512), BF16),
        pltpu.VMEM((2, Z, 3, K, 128), BF16),
        pltpu.VMEM((2, Z, 3, K, 128), BF16),
        pltpu.VMEM((2, Z, K, 128), BF16),
        pltpu.VMEM((2, Z, K, 128), BF16),
        pltpu.VMEM((K, 128), F32),
        pltpu.VMEM((2, 2, X, 128, 128), F32),
        pltpu.VMEM((2, 2, X - 1, 128, 128), F32),
        dma((4,)),
        *pair(2, 2, Y - 1),
        *pair(2, 2, 2, 3),
        *pair(2, 2),
        *pair(2, 2, Y - 1),
        *pair(2, 2, Z),
        *pair(2, Z),
        *pair(2, Z, 3),
        *pair(2, Z),
        *pair(2, 2, X - 1),
        *pair(2, 2, X - 1),
    ]
    held = pl.pallas_call(
        kernel,
        out_shape=jax.ShapeDtypeStruct((2, 2, X, 128, 128), BF16),
        in_specs=[vmem, pl.BlockSpec(memory_space=pl.ANY), vmem, vmem],
        out_specs=vmem,
        scratch_shapes=scratch,
        compiler_params=pltpu.CompilerParams(
            collective_id=0, has_side_effects=True, vmem_limit_bytes=60 * 1024 * 1024
        ),
    )(density_panel, blocks, block_row, block_slot)
    return pl.pallas_call(
        lay_out, out_shape=(shape, shape), in_specs=[vmem], out_specs=(vmem, vmem)
    )(held)


def solution(mesh):
    in_specs = (
        P("row", None),
        P(("row", "col"), None),
        P(("row", "col")),
        P(("row", "col")),
        P(("row", "col"), None),
    )
    out_specs = (P("row", None), P("row", None))
    return jax.shard_map(
        per_device, mesh=mesh, in_specs=in_specs, out_specs=out_specs, check_vma=False
    )
```

```python
import jax
import jax.numpy as jnp
from jax import lax
from jax.experimental import pallas as pl
from jax.experimental.pallas import tpu as pltpu
from jax.sharding import PartitionSpec as P

B = 64
K = 256
Z, Y, C, X = 8, 4, 2, 4
BF16, F32 = jnp.bfloat16, jnp.float32
RELAY, SUMMED, DIRECT = 0, 1, 2
FIRST_AFTER = 3


def kernel(
    panel, blocks, block_row, block_slot, out,
    stored, matrix, pick, perm, pt, gathered, acc, held, own,
    core_out, core_in, y_out, y_in, z_out, z_in, z_own, x_out, x_in,
    fetch, ay_s, ay_r, az_s, az_r, af_s, af_r, ag_s, ag_r, ac_s, ac_r, rc_s, rc_r, ry_s, ry_r, rz_s, rz_r, xr_s, xr_r, xg_s, xg_r,
):
    row, x = lax.axis_index("row"), lax.axis_index("col")
    z, y, k = row // (Y * C), (row // C) % Y, row % C
    ahead, behind, across = (y + 1 + 2 * k) % Y, (y + 3 + 2 * k) % Y, (y + 2) % Y

    def at(zz, yy, kk):
        return (zz * Y + yy) * C + kk

    def copy(src, dst, send, recv, to_row, to_col=None):
        return pltpu.make_async_remote_copy(
            src_ref=src, dst_ref=dst, send_sem=send, recv_sem=recv,
            device_id=(to_row, x if to_col is None else to_col),
            device_id_type=pl.DeviceIdType.MESH,
        )

    def load(part):
        lanes = pl.ds(pl.multiple_of(part * 1024, 1024), 1024)
        return pltpu.make_async_copy(blocks.at[:, lanes], stored.at[:, lanes], fetch.at[part])

    for part in range(4):
        load(part).start()
    barrier = pltpu.get_barrier_semaphore()

    def greet(to_row, to_col):
        pl.semaphore_signal(barrier, inc=1, device_id=(to_row, to_col), device_id_type=pl.DeviceIdType.MESH)

    greet(at(z, y, 1 - k), x)
    for d in range(1, Y):
        greet(at(z, (y + d) % Y, k), x)
    for d in range(1, Z):
        greet(at((z + d) % Z, y, k), x)
    for d in range(1, X):
        greet(row, (x + d) % X)

    for h in range(2):
        for c in range(X):
            for t in range(2):
                held[0, h, c, t * 64:(t + 1) * 64, :] = panel[
                    (c + 4 * t) * 64:(c + 4 * t + 1) * 64, h * 128:(h + 1) * 128
                ]

    def set_up():
        slot = block_slot[...]
        chunk_of = ((slot // 16) * C + (slot // 2) % 2) * Y + (slot // 4) % 4
        place = jnp.where(slot >= 0, chunk_of * 16 + (slot % 2) * 8 + block_row[...], -1)
        r = lax.broadcasted_iota(jnp.int32, (512, 384), 0)
        want = (r // 8) * 16 + r % 8
        at_place = jnp.broadcast_to(place, (512, 384))
        pick[:, 0:384] = jnp.where(at_place == want, 1.0, 0.0).astype(BF16)
        pick[:, 384:768] = jnp.where(at_place == want + 8, 1.0, 0.0).astype(BF16)
        j = lax.broadcasted_iota(jnp.int32, (512, 512), 0)
        q = lax.broadcasted_iota(jnp.int32, (512, 512), 1)
        i, a = j % 8, j // 8
        perm[...] = jnp.where(q == ((i % 4) * 2 + i // 4) * 64 + a, 1.0, 0.0).astype(BF16)

    def build(step, half):
        tile = stored[:, pl.ds(pl.multiple_of(step * 128, 128), 128)].astype(F32)
        turned = pltpu.roll(tile, 64, 1)
        low = lax.broadcasted_iota(jnp.int32, (384, 128), 1) < 64
        upper = jnp.concatenate([jnp.where(low, tile, 0.0), jnp.where(low, turned, 0.0)], axis=1)
        lower = jnp.concatenate([jnp.where(low, 0.0, turned), jnp.where(low, 0.0, tile)], axis=1)
        both = jnp.concatenate([upper, lower], axis=0).astype(BF16)
        placed = jnp.dot(pick[half * 256:(half + 1) * 256, :], both, preferred_element_type=F32)
        first = placed[:, 0:128].reshape(32, 8, 128)
        second = placed[:, 128:256].reshape(32, 8, 128)
        rows = jnp.concatenate([first, second], axis=1).astype(BF16)
        for chunk in range(32):
            start = (half * 32 + chunk) * 128
            matrix[pl.ds(pl.multiple_of(step * 16, 16), 16), start:start + 128] = rows[chunk]

    def ag_y(p, h, d):
        part = gathered.at[p, h, z, k, pl.ds(pl.multiple_of(y * 128, 128), 128)]
        return copy(part, part, ay_s.at[p, h, d - 1], ay_r.at[p, h, d - 1], at(z, (y + d) % Y, k))

    def ag_z(p, h, way, s, zo, to):
        unit = gathered.at[p, h, zo, k]
        return copy(unit, unit, az_s.at[p, h, way, s - 1], az_r.at[p, h, way, s - 1], at(to, y, k))

    def ag_core(p, h, zo, kk):
        unit = gathered.at[p, h, zo, kk]
        return copy(unit, unit, ac_s.at[p, h, zo], ac_r.at[p, h, zo], at(z, y, 1 - k))

    def rs_core(p, zo):
        return copy(core_out.at[p, zo], core_in.at[p, zo], rc_s.at[p, zo], rc_r.at[p, zo], at(z, y, 1 - k))

    def rs_y(p, zo, what):
        to = behind if what == DIRECT else ahead
        return copy(y_out.at[p, zo, what], y_in.at[p, zo, what], ry_s.at[p, zo, what], ry_r.at[p, zo, what], at(z, to, k))

    def rs_z(p, zo, frm):
        return copy(z_out.at[p, zo], z_in.at[p, frm], rz_s.at[p, zo], rz_r.at[p, frm], at(zo, y, k))

    def rs_x(p, h, d):
        to = (x + d) % X
        return copy(x_out.at[p, h, to], x_in.at[p, h, d - 1], xr_s.at[p, h, d - 1], xr_r.at[p, h, d - 1], row, to)

    def ag_x(p, h, d, frm):
        part = held.at[p + 1, h, frm]
        return copy(part, part, xg_s.at[p, h, d - 1], xg_r.at[p, h, d - 1], row, (x + d) % X)

    def ag_far(p, h, zo, to):
        part = gathered.at[p, h, zo, k, pl.ds(pl.multiple_of(y * 128, 128), 128)]
        return copy(part, part, af_s.at[p, h], af_r.at[p, h], at(to, y, k))

    def ag_far_y(p, h, d):
        part = gathered.at[p, h, z + 4, k, pl.ds(pl.multiple_of(y * 128, 128), 128)]
        return copy(part, part, ag_s.at[p, h, d - 1], ag_r.at[p, h, d - 1], at(z, (y + d) % Y, k))

    def ring_send(way, s):
        down = (z >= 1) & (z + s - 1 <= 7) & (s <= 3)
        up_zo = (z + 9 - s) % 8
        up = (up_zo >= 5) & (s <= 3)
        if way == 0:
            return down, z + s - 1, z - 1
        return up, up_zo, (z + 1) % 8

    def ring_get(way, s):
        if way == 0:
            return (z + s <= 7) & (s <= 3), z + s
        zo = (z + 8 - s) % 8
        return (zo >= 5) & (s <= 3), zo

    def columns(zo, kk):
        return pl.ds(pl.multiple_of((zo * C + kk) * 512, 512), 512)

    def direct_both(p, zo, kk):
        wide = jnp.concatenate([gathered[p, 0, zo, kk], gathered[p, 1, zo, kk]], axis=1)
        part = jnp.dot(matrix[:, columns(zo, kk)], wide, preferred_element_type=F32)
        for h in range(2):
            acc[h] += part[:, h * 128:(h + 1) * 128]

    def direct_half(p, h, zo, kk):
        acc[h] += jnp.dot(matrix[:, columns(zo, kk)], gathered[p, h, zo, kk], preferred_element_type=F32)

    def ag_start(p, h):
        gathered[p, h, z, k, pl.ds(pl.multiple_of(y * 128, 128), 128), :] = held[p, h, x]
        for d in range(1, Y):
            ag_y(p, h, d).start()

        @pl.when(z >= 4)
        def _():
            ag_far(p, h, z, z - 4).start()

    def ag_pass(p, h, s):
        for way in range(2):
            cond, zo, to = ring_send(way, s)

            @pl.when(cond)
            def _():
                ag_z(p, h, way, s, zo, to).start()

    def ag_first(p, h):
        for d in range(1, Y):
            ag_y(p, h, d).wait_recv()
        ag_pass(p, h, 1)
        ag_core(p, h, z, k).start()

    def far_pass(p):
        @pl.when(z < 4)
        def _():
            for h in range(2):
                ag_far(p, h, z + 4, z).wait_recv()
                for d in range(1, Y):
                    ag_far_y(p, h, d).start()

    def far_core(p):
        @pl.when(z < 4)
        def _():
            for h in range(2):
                for d in range(1, Y):
                    ag_far_y(p, h, d).wait_recv()
                ag_core(p, h, z + 4, k).start()

    def far_use(p):
        @pl.when(z < 4)
        def _():
            direct_both(p, z + 4, k)
            for h in range(2):
                ag_core(p, h, z + 4, 1 - k).wait_recv()
            direct_both(p, z + 4, 1 - k)

    def ag_own(p):
        acc[...] = jnp.zeros_like(acc)

        def use(kk, carry):
            @pl.when(kk != k)
            def _():
                for h in range(2):
                    ag_core(p, h, z, kk).wait_recv()

            direct_both(p, z, kk)
            return carry

        lax.fori_loop(0, C, use, 0)

    def ag_step(p, e):
        s, h = 1 + e // 2, e % 2
        for way in range(2):
            cond, zo = ring_get(way, s)

            @pl.when(cond)
            def _():
                ag_z(p, h, way, s, zo, z).wait_recv()

        @pl.when(s < 3)
        def _():
            ag_pass(p, h, s + 1)

        for way in range(2):
            cond, zo = ring_get(way, s)

            @pl.when(cond & (zo > z))
            def _():
                ag_core(p, h, zo, k).start()

    def ag_use(p, e, mine):
        s, h = 1 + e // 2, e % 2

        def use(way, carry):
            kk = k if mine else 1 - k
            down, zd = ring_get(0, s)
            up, zu = ring_get(1, s)
            zo = jnp.where(way == 0, zd, zu)
            cond = ((way == 0) & down | (way == 1) & up) & (zo > z)

            @pl.when(cond)
            def _():
                if not mine:
                    ag_core(p, h, zo, kk).wait_recv()

                @pl.when(s == 3)
                def _():
                    direct_half(p, h, zo, kk)

                @pl.when((s < 3) & (h == 1))
                def _():
                    direct_both(p, zo, kk)

            return carry

        lax.fori_loop(0, 2, use, 0)

    def make_pt(p):
        for h in range(2):
            ordered = jnp.dot(perm[...], held[p, h].reshape(512, 128), preferred_element_type=F32)
            pt[h * 128:(h + 1) * 128, :] = ordered.T.astype(BF16)

    def mirror(zo, kk):
        return jnp.dot(pt[...], matrix[:, columns(zo, kk)], preferred_element_type=F32)

    def rs_a(p, zo):
        core_out[p, zo] = mirror(zo, 1 - k).astype(BF16)
        rs_core(p, zo).start()

    def rs_b1(p, zo):
        part = mirror(zo, k)
        rs_core(p, zo).wait_recv()
        part = part + core_in[p, zo].astype(F32)
        for to in range(Y):
            own[zo, to] = part[:, to * 128:(to + 1) * 128]
        y_out[p, zo, RELAY] = own[zo, across].astype(BF16)
        rs_y(p, zo, RELAY).start()
        y_out[p, zo, DIRECT] = own[zo, behind].astype(BF16)
        rs_y(p, zo, DIRECT).start()

    def rs_b2(p, zo):
        rs_y(p, zo, RELAY).wait_recv()
        y_out[p, zo, SUMMED] = (own[zo, ahead] + y_in[p, zo, RELAY].astype(F32)).astype(BF16)
        rs_y(p, zo, SUMMED).start()

    def rs_c(p, zo):
        rs_y(p, zo, DIRECT).wait_recv()
        rs_y(p, zo, SUMMED).wait_recv()
        total = own[zo, y] + y_in[p, zo, DIRECT].astype(F32) + y_in[p, zo, SUMMED].astype(F32)

        @pl.when(zo > z)
        def _():
            z_out[p, zo] = total.astype(BF16)

            @pl.when(jnp.logical_not(waits(zo)))
            def _():
                rs_z(p, zo, z).start()

        @pl.when(zo == z)
        def _():
            z_own[...] = total

    def waits(zo):
        return (z >= 1) & (zo - z >= 4)

    def rs_late(p):
        for zo in range(5, Z):
            @pl.when(waits(zo))
            def _():
                rs_z(p, zo, z).start()

    def rs_d(p):
        def add(zi, carry):
            rs_z(p, zi, zi).wait_recv()
            z_own[...] += z_in[p, zi].astype(F32)
            return carry

        lax.fori_loop(0, z, add, 0)

    def x_start(p, h):
        for c in range(X):
            for t in range(2):
                x_out[p, h, c, t * 64:(t + 1) * 64, :] = acc[h, pl.ds(c + 4 * t, 64, stride=8), :]
        for d in range(1, X):
            rs_x(p, h, d).start()

    def finish(p, h):
        total = x_out[p, h, x] + z_own[h * 128:(h + 1) * 128, :].T
        for d in range(1, X):
            rs_x(p, h, d).wait_recv()
            total = total + x_in[p, h, d - 1]
        held[p + 1, h, x] = total.astype(BF16)
        for d in range(1, X):
            ag_x(p, h, d, x).start()

    def collect(p):
        for h in range(2):
            for d in range(1, X):
                ag_x(p, h, d, (x + X - d) % X).wait_recv()
        out[p] = held[p + 1]

    def build_rest(e):
        def build_some(part, carry):
            for n in range(4):
                build(part * 4 + n, 0)
            return carry

        @pl.when(z < 4)
        def _():
            lax.fori_loop(e * 4, e * 4 + 4, build_some, 0)

    def product(p, carry):
        for h in range(2):
            ag_start(p, h)

        @pl.when(p == 0)
        def _():
            set_up()

            def build_some(part, carry):
                @pl.when(part % 2 == 0)
                def _():
                    load(part // 2).wait()

                for n in range(4):
                    build(part * 4 + n, 1)

                @pl.when(part == FIRST_AFTER)
                def _():
                    for h in range(2):
                        ag_first(p, h)

                return carry

            lax.fori_loop(0, 8, build_some, 0)

        @pl.when(p == 1)
        def _():
            for h in range(2):
                ag_first(p, h)
            collect(0)

        make_pt(p)
        lead = jnp.where(p == 0, -2, 0)
        use = 1 - p

        def turn(step, carry):
            n = step - 3

            def stage(first, body, count):
                @pl.when((n >= first) & (n < first + count))
                def _():
                    body(n - first)

            def stage_zo(first, body):
                zo = 7 - (n - first)

                @pl.when((n >= first) & (zo >= z))
                def _():
                    body(p, zo)

            stage_zo(-3, rs_a)
            stage_zo(-1, rs_b1)
            stage(lead, lambda e: ag_step(p, e), 6)
            stage(jnp.where(p == 0, -3, -2), lambda e: far_pass(p), 1)
            stage_zo(1, rs_b2)
            stage_zo(3, rs_c)
            stage(jnp.where(p == 0, -1, 1), lambda e: far_core(p), 1)
            stage(jnp.where(p == 0, -1, 99), build_rest, 2)
            stage(1 - 2 * p, lambda e: ag_own(p), 1)
            stage(2, lambda e: far_use(p), 1)
            stage(use, lambda e: ag_use(p, e, True), 6)
            stage(use + 1, lambda e: ag_use(p, e, False), 6)
            stage(use + 5, lambda e: x_start(p, e), 2)
            stage(jnp.where(p == 0, 6, 7), lambda e: rs_late(p), 1)
            return carry

        lax.fori_loop(0, 14, turn, 0)
        rs_d(p)
        for h in range(2):
            finish(p, h)
        return carry

    pl.semaphore_wait(barrier, 1 + (Y - 1) + (Z - 1) + (X - 1))
    lax.fori_loop(0, 2, product, 0)

    def left(p, carry):
        for h in range(2):
            for d in range(1, Y):
                ag_y(p, h, d).wait_send()

            @pl.when(z >= 4)
            def _():
                ag_far(p, h, z, z - 4).wait_send()

            @pl.when(z < 4)
            def _():
                for d in range(1, Y):
                    ag_far_y(p, h, d).wait_send()

            for d in range(1, X):
                rs_x(p, h, d).wait_send()
                ag_x(p, h, d, x).wait_send()
            for way in range(2):
                for s in range(1, 4):
                    cond, zo, to = ring_send(way, s)

                    @pl.when(cond)
                    def _():
                        ag_z(p, h, way, s, zo, to).wait_send()

        def left_zo(zo, carry):
            for h in range(2):
                ag_core(p, h, zo, k).wait_send()
            rs_core(p, zo).wait_send()
            for what in (RELAY, SUMMED, DIRECT):
                rs_y(p, zo, what).wait_send()

            @pl.when(zo > z)
            def _():
                rs_z(p, zo, z).wait_send()

            return carry

        lax.fori_loop(z, Z, left_zo, 0)
        return carry

    lax.fori_loop(0, 2, left, 0)
    collect(1)


def lay_out(held, out1, out2):
    for p, out in enumerate((out1, out2)):
        for h in range(2):
            for c in range(X):
                for t in range(2):
                    out[(c + 4 * t) * 64:(c + 4 * t + 1) * 64, h * 128:(h + 1) * 128] = held[
                        p, h, c, t * 64:(t + 1) * 64, :
                    ]


def per_device(density_panel, blocks, block_row, block_slot, requests):
    vmem = pl.BlockSpec(memory_space=pltpu.VMEM)
    dma = pltpu.SemaphoreType.DMA
    shape = jax.ShapeDtypeStruct((512, K), BF16)

    def pair(*dims):
        return [dma(dims), dma(dims)]

    scratch = [
        pltpu.VMEM((384, 4096), BF16),
        pltpu.VMEM((512, 8192), BF16),
        pltpu.VMEM((512, 768), BF16),
        pltpu.VMEM((512, 512), BF16),
        pltpu.VMEM((256, 512), BF16),
        pltpu.VMEM((2, 2, Z, C, 512, 128), BF16),
        pltpu.VMEM((2, 512, 128), F32),
        pltpu.VMEM((3, 2, X, 128, 128), BF16),
        pltpu.VMEM((Z, Y, K, 128), F32),
        pltpu.VMEM((2, Z, K, 512), BF16),
        pltpu.VMEM((2, Z, K, 512), BF16),
        pltpu.VMEM((2, Z, 3, K, 128), BF16),
        pltpu.VMEM((2, Z, 3, K, 128), BF16),
        pltpu.VMEM((2, Z, K, 128), BF16),
        pltpu.VMEM((2, Z, K, 128), BF16),
        pltpu.VMEM((K, 128), F32),
        pltpu.VMEM((2, 2, X, 128, 128), F32),
        pltpu.VMEM((2, 2, X - 1, 128, 128), F32),
        dma((4,)),
        *pair(2, 2, Y - 1),
        *pair(2, 2, 2, 3),
        *pair(2, 2),
        *pair(2, 2, Y - 1),
        *pair(2, 2, Z),
        *pair(2, Z),
        *pair(2, Z, 3),
        *pair(2, Z),
        *pair(2, 2, X - 1),
        *pair(2, 2, X - 1),
    ]
    held = pl.pallas_call(
        kernel,
        out_shape=jax.ShapeDtypeStruct((2, 2, X, 128, 128), BF16),
        in_specs=[vmem, pl.BlockSpec(memory_space=pl.ANY), vmem, vmem],
        out_specs=vmem,
        scratch_shapes=scratch,
        compiler_params=pltpu.CompilerParams(
            collective_id=0, has_side_effects=True, vmem_limit_bytes=60 * 1024 * 1024
        ),
    )(density_panel, blocks, block_row, block_slot)
    return pl.pallas_call(
        lay_out, out_shape=(shape, shape), in_specs=[vmem], out_specs=(vmem, vmem)
    )(held)


def solution(mesh):
    in_specs = (
        P("row", None),
        P(("row", "col"), None),
        P(("row", "col")),
        P(("row", "col")),
        P(("row", "col"), None),
    )
    out_specs = (P("row", None), P("row", None))
    return jax.shard_map(
        per_device, mesh=mesh, in_specs=in_specs, out_specs=out_specs, check_vma=False
    )
```

```python
import jax
import jax.numpy as jnp
from jax import lax
from jax.experimental import pallas as pl
from jax.experimental.pallas import tpu as pltpu
from jax.sharding import PartitionSpec as P

B = 64
K = 256
Z, Y, C, X = 8, 4, 2, 4
BF16, F32 = jnp.bfloat16, jnp.float32
RELAY, SUMMED, DIRECT = 0, 1, 2
FIRST_AFTER = 3


def kernel(
    panel, blocks, block_row, block_slot, out,
    stored, matrix, pick, perm, pt, gathered, acc, held, own,
    core_out, core_in, y_out, y_in, z_out, z_in, z_own, x_out, x_in,
    fetch, ay_s, ay_r, az_s, az_r, af_s, af_r, ag_s, ag_r, ac_s, ac_r, rc_s, rc_r, ry_s, ry_r, rz_s, rz_r, xr_s, xr_r, xg_s, xg_r,
):
    row, x = lax.axis_index("row"), lax.axis_index("col")
    z, y, k = row // (Y * C), (row // C) % Y, row % C
    ahead, behind, across = (y + 1 + 2 * k) % Y, (y + 3 + 2 * k) % Y, (y + 2) % Y

    def at(zz, yy, kk):
        return (zz * Y + yy) * C + kk

    def copy(src, dst, send, recv, to_row, to_col=None):
        return pltpu.make_async_remote_copy(
            src_ref=src, dst_ref=dst, send_sem=send, recv_sem=recv,
            device_id=(to_row, x if to_col is None else to_col),
            device_id_type=pl.DeviceIdType.MESH,
        )

    def load(part):
        lanes = pl.ds(pl.multiple_of(part * 1024, 1024), 1024)
        return pltpu.make_async_copy(blocks.at[:, lanes], stored.at[:, lanes], fetch.at[part])

    for part in range(4):
        load(part).start()
    barrier = pltpu.get_barrier_semaphore()

    def greet(to_row, to_col):
        pl.semaphore_signal(barrier, inc=1, device_id=(to_row, to_col), device_id_type=pl.DeviceIdType.MESH)

    greet(at(z, y, 1 - k), x)
    for d in range(1, Y):
        greet(at(z, (y + d) % Y, k), x)
    for d in range(1, Z):
        greet(at((z + d) % Z, y, k), x)
    for d in range(1, X):
        greet(row, (x + d) % X)

    for h in range(2):
        for c in range(X):
            for t in range(2):
                held[0, h, c, t * 64:(t + 1) * 64, :] = panel[
                    (c + 4 * t) * 64:(c + 4 * t + 1) * 64, h * 128:(h + 1) * 128
                ]

    def set_up():
        slot = block_slot[...]
        chunk_of = ((slot // 16) * C + (slot // 2) % 2) * Y + (slot // 4) % 4
        place = jnp.where(slot >= 0, chunk_of * 16 + (slot % 2) * 8 + block_row[...], -1)
        r = lax.broadcasted_iota(jnp.int32, (512, 384), 0)
        want = (r // 8) * 16 + r % 8
        at_place = jnp.broadcast_to(place, (512, 384))
        pick[:, 0:384] = jnp.where(at_place == want, 1.0, 0.0).astype(BF16)
        pick[:, 384:768] = jnp.where(at_place == want + 8, 1.0, 0.0).astype(BF16)
        j = lax.broadcasted_iota(jnp.int32, (512, 512), 0)
        q = lax.broadcasted_iota(jnp.int32, (512, 512), 1)
        i, a = j % 8, j // 8
        perm[...] = jnp.where(q == ((i % 4) * 2 + i // 4) * 64 + a, 1.0, 0.0).astype(BF16)

    def build(step, half):
        tile = stored[:, pl.ds(pl.multiple_of(step * 128, 128), 128)].astype(F32)
        turned = pltpu.roll(tile, 64, 1)
        low = lax.broadcasted_iota(jnp.int32, (384, 128), 1) < 64
        upper = jnp.concatenate([jnp.where(low, tile, 0.0), jnp.where(low, turned, 0.0)], axis=1)
        lower = jnp.concatenate([jnp.where(low, 0.0, turned), jnp.where(low, 0.0, tile)], axis=1)
        both = jnp.concatenate([upper, lower], axis=0).astype(BF16)
        placed = jnp.dot(pick[half * 256:(half + 1) * 256, :], both, preferred_element_type=F32)
        first = placed[:, 0:128].reshape(32, 8, 128)
        second = placed[:, 128:256].reshape(32, 8, 128)
        rows = jnp.concatenate([first, second], axis=1).astype(BF16)
        for chunk in range(32):
            start = (half * 32 + chunk) * 128
            matrix[pl.ds(pl.multiple_of(step * 16, 16), 16), start:start + 128] = rows[chunk]

    def ag_y(p, h, d):
        part = gathered.at[p, h, z, k, pl.ds(pl.multiple_of(y * 128, 128), 128)]
        return copy(part, part, ay_s.at[p, h, d - 1], ay_r.at[p, h, d - 1], at(z, (y + d) % Y, k))

    def ag_z(p, h, way, s, zo, to):
        unit = gathered.at[p, h, zo, k]
        return copy(unit, unit, az_s.at[p, h, way, s - 1], az_r.at[p, h, way, s - 1], at(to, y, k))

    def ag_core(p, h, zo, kk):
        unit = gathered.at[p, h, zo, kk]
        return copy(unit, unit, ac_s.at[p, h, zo], ac_r.at[p, h, zo], at(z, y, 1 - k))

    def rs_core(p, zo):
        return copy(core_out.at[p, zo], core_in.at[p, zo], rc_s.at[p, zo], rc_r.at[p, zo], at(z, y, 1 - k))

    def rs_y(p, zo, what):
        to = behind if what == DIRECT else ahead
        return copy(y_out.at[p, zo, what], y_in.at[p, zo, what], ry_s.at[p, zo, what], ry_r.at[p, zo, what], at(z, to, k))

    def rs_z(p, zo, frm):
        return copy(z_out.at[p, zo], z_in.at[p, frm], rz_s.at[p, zo], rz_r.at[p, frm], at(zo, y, k))

    def rs_x(p, h, d):
        to = (x + d) % X
        return copy(x_out.at[p, h, to], x_in.at[p, h, d - 1], xr_s.at[p, h, d - 1], xr_r.at[p, h, d - 1], row, to)

    def ag_x(p, h, d, frm):
        part = held.at[p + 1, h, frm]
        return copy(part, part, xg_s.at[p, h, d - 1], xg_r.at[p, h, d - 1], row, (x + d) % X)

    def ag_far(p, h, zo, to):
        part = gathered.at[p, h, zo, k, pl.ds(pl.multiple_of(y * 128, 128), 128)]
        return copy(part, part, af_s.at[p, h], af_r.at[p, h], at(to, y, k))

    def ag_far_y(p, h, d):
        part = gathered.at[p, h, z + 4, k, pl.ds(pl.multiple_of(y * 128, 128), 128)]
        return copy(part, part, ag_s.at[p, h, d - 1], ag_r.at[p, h, d - 1], at(z, (y + d) % Y, k))

    def ring_send(way, s):
        down = (z >= 1) & (z + s - 1 <= 7) & (s <= 3)
        up_zo = (z + 9 - s) % 8
        up = (up_zo >= 5) & (s <= 3)
        if way == 0:
            return down, z + s - 1, z - 1
        return up, up_zo, (z + 1) % 8

    def ring_get(way, s):
        if way == 0:
            return (z + s <= 7) & (s <= 3), z + s
        zo = (z + 8 - s) % 8
        return (zo >= 5) & (s <= 3), zo

    def columns(zo, kk):
        return pl.ds(pl.multiple_of((zo * C + kk) * 512, 512), 512)

    def direct_both(p, zo, kk):
        wide = jnp.concatenate([gathered[p, 0, zo, kk], gathered[p, 1, zo, kk]], axis=1)
        part = jnp.dot(matrix[:, columns(zo, kk)], wide, preferred_element_type=F32)
        for h in range(2):
            acc[h] += part[:, h * 128:(h + 1) * 128]

    def direct_half(p, h, zo, kk):
        acc[h] += jnp.dot(matrix[:, columns(zo, kk)], gathered[p, h, zo, kk], preferred_element_type=F32)

    def ag_start(p, h):
        gathered[p, h, z, k, pl.ds(pl.multiple_of(y * 128, 128), 128), :] = held[p, h, x]
        for d in range(1, Y):
            ag_y(p, h, d).start()

        @pl.when(z >= 4)
        def _():
            ag_far(p, h, z, z - 4).start()

    def ag_pass(p, h, s):
        for way in range(2):
            cond, zo, to = ring_send(way, s)

            @pl.when(cond)
            def _():
                ag_z(p, h, way, s, zo, to).start()

    def ag_first(p, h):
        for d in range(1, Y):
            ag_y(p, h, d).wait_recv()
        ag_pass(p, h, 1)
        ag_core(p, h, z, k).start()

    def far_pass(p):
        @pl.when(z < 4)
        def _():
            for h in range(2):
                ag_far(p, h, z + 4, z).wait_recv()
                for d in range(1, Y):
                    ag_far_y(p, h, d).start()

    def far_core(p):
        @pl.when(z < 4)
        def _():
            for h in range(2):
                for d in range(1, Y):
                    ag_far_y(p, h, d).wait_recv()
                ag_core(p, h, z + 4, k).start()

    def far_use(p):
        @pl.when(z < 4)
        def _():
            direct_both(p, z + 4, k)
            for h in range(2):
                ag_core(p, h, z + 4, 1 - k).wait_recv()
            direct_both(p, z + 4, 1 - k)

    def ag_own(p):
        acc[...] = jnp.zeros_like(acc)

        def use(kk, carry):
            @pl.when(kk != k)
            def _():
                for h in range(2):
                    ag_core(p, h, z, kk).wait_recv()

            direct_both(p, z, kk)
            return carry

        lax.fori_loop(0, C, use, 0)

    def ag_step(p, e):
        s, h = 1 + e // 2, e % 2
        for way in range(2):
            cond, zo = ring_get(way, s)

            @pl.when(cond)
            def _():
                ag_z(p, h, way, s, zo, z).wait_recv()

        @pl.when(s < 3)
        def _():
            ag_pass(p, h, s + 1)

        for way in range(2):
            cond, zo = ring_get(way, s)

            @pl.when(cond & (zo > z))
            def _():
                ag_core(p, h, zo, k).start()

    def ag_use(p, e, mine):
        s, h = 1 + e // 2, e % 2

        def use(way, carry):
            kk = k if mine else 1 - k
            down, zd = ring_get(0, s)
            up, zu = ring_get(1, s)
            zo = jnp.where(way == 0, zd, zu)
            cond = ((way == 0) & down | (way == 1) & up) & (zo > z)

            @pl.when(cond)
            def _():
                if not mine:
                    ag_core(p, h, zo, kk).wait_recv()

                @pl.when(s == 3)
                def _():
                    direct_half(p, h, zo, kk)

                @pl.when((s < 3) & (h == 1))
                def _():
                    direct_both(p, zo, kk)

            return carry

        lax.fori_loop(0, 2, use, 0)

    def make_pt(p):
        for h in range(2):
            ordered = jnp.dot(perm[...], held[p, h].reshape(512, 128), preferred_element_type=F32)
            pt[h * 128:(h + 1) * 128, :] = ordered.T.astype(BF16)

    def mirror(zo, kk):
        return jnp.dot(pt[...], matrix[:, columns(zo, kk)], preferred_element_type=F32)

    def rs_a(p, zo):
        core_out[p, zo] = mirror(zo, 1 - k).astype(BF16)
        rs_core(p, zo).start()

    def rs_b1(p, zo):
        part = mirror(zo, k)
        rs_core(p, zo).wait_recv()
        part = part + core_in[p, zo].astype(F32)
        for to in range(Y):
            own[zo, to] = part[:, to * 128:(to + 1) * 128]
        y_out[p, zo, RELAY] = own[zo, across].astype(BF16)
        rs_y(p, zo, RELAY).start()
        y_out[p, zo, DIRECT] = own[zo, behind].astype(BF16)
        rs_y(p, zo, DIRECT).start()

    def rs_b2(p, zo):
        rs_y(p, zo, RELAY).wait_recv()
        y_out[p, zo, SUMMED] = (own[zo, ahead] + y_in[p, zo, RELAY].astype(F32)).astype(BF16)
        rs_y(p, zo, SUMMED).start()

    def rs_c(p, zo):
        rs_y(p, zo, DIRECT).wait_recv()
        rs_y(p, zo, SUMMED).wait_recv()
        total = own[zo, y] + y_in[p, zo, DIRECT].astype(F32) + y_in[p, zo, SUMMED].astype(F32)

        @pl.when(zo > z)
        def _():
            z_out[p, zo] = total.astype(BF16)

            @pl.when(jnp.logical_not(waits(zo)))
            def _():
                rs_z(p, zo, z).start()

        @pl.when(zo == z)
        def _():
            z_own[...] = total

    def waits(zo):
        return (z >= 1) & (zo - z >= 4)

    def rs_late(p):
        for zo in range(5, Z):
            @pl.when(waits(zo))
            def _():
                rs_z(p, zo, z).start()

    def rs_d(p):
        def add(zi, carry):
            rs_z(p, zi, zi).wait_recv()
            z_own[...] += z_in[p, zi].astype(F32)
            return carry

        lax.fori_loop(0, z, add, 0)

    def x_start(p, h):
        for c in range(X):
            for t in range(2):
                x_out[p, h, c, t * 64:(t + 1) * 64, :] = acc[h, pl.ds(c + 4 * t, 64, stride=8), :]
        for d in range(1, X):
            rs_x(p, h, d).start()

    def finish(p, h):
        total = x_out[p, h, x] + z_own[h * 128:(h + 1) * 128, :].T
        for d in range(1, X):
            rs_x(p, h, d).wait_recv()
            total = total + x_in[p, h, d - 1]
        held[p + 1, h, x] = total.astype(BF16)
        for d in range(1, X):
            ag_x(p, h, d, x).start()

    def collect(p):
        for h in range(2):
            for d in range(1, X):
                ag_x(p, h, d, (x + X - d) % X).wait_recv()
        out[p] = held[p + 1]

    def build_rest(e):
        def build_some(part, carry):
            for n in range(4):
                build(part * 4 + n, 0)
            return carry

        @pl.when(z < 4)
        def _():
            lax.fori_loop(e * 4, e * 4 + 4, build_some, 0)

    def product(p, carry):
        for h in range(2):
            ag_start(p, h)

        @pl.when(p == 0)
        def _():
            set_up()

            def build_some(part, carry):
                @pl.when(part % 2 == 0)
                def _():
                    load(part // 2).wait()

                for n in range(4):
                    build(part * 4 + n, 1)

                @pl.when(part == FIRST_AFTER)
                def _():
                    for h in range(2):
                        ag_first(p, h)

                return carry

            lax.fori_loop(0, 8, build_some, 0)

        @pl.when(p == 1)
        def _():
            for h in range(2):
                ag_first(p, h)
            collect(0)

        make_pt(p)
        lead = jnp.where(p == 0, -2, 0)
        use = 1 - p

        def turn(step, carry):
            n = step - 3

            def stage(first, body, count):
                @pl.when((n >= first) & (n < first + count))
                def _():
                    body(n - first)

            def stage_zo(first, body):
                zo = 7 - (n - first)

                @pl.when((n >= first) & (zo >= z))
                def _():
                    body(p, zo)

            stage_zo(-3, rs_a)
            stage_zo(-1, rs_b1)
            stage(lead, lambda e: ag_step(p, e), 6)
            stage(jnp.where(p == 0, -3, -2), lambda e: far_pass(p), 1)
            stage_zo(1, rs_b2)
            stage_zo(3, rs_c)
            stage(jnp.where(p == 0, -1, 1), lambda e: far_core(p), 1)
            stage(jnp.where(p == 0, -2, 99), build_rest, 2)
            stage(1 - 2 * p, lambda e: ag_own(p), 1)
            stage(2, lambda e: far_use(p), 1)
            stage(use, lambda e: ag_use(p, e, True), 6)
            stage(use + 1, lambda e: ag_use(p, e, False), 6)
            stage(use + 5, lambda e: x_start(p, e), 2)
            stage(jnp.where(p == 0, 5, 6), lambda e: rs_late(p), 1)
            return carry

        lax.fori_loop(0, 14, turn, 0)
        rs_d(p)
        for h in range(2):
            finish(p, h)
        return carry

    pl.semaphore_wait(barrier, 1 + (Y - 1) + (Z - 1) + (X - 1))
    lax.fori_loop(0, 2, product, 0)

    def left(p, carry):
        for h in range(2):
            for d in range(1, Y):
                ag_y(p, h, d).wait_send()

            @pl.when(z >= 4)
            def _():
                ag_far(p, h, z, z - 4).wait_send()

            @pl.when(z < 4)
            def _():
                for d in range(1, Y):
                    ag_far_y(p, h, d).wait_send()

            for d in range(1, X):
                rs_x(p, h, d).wait_send()
                ag_x(p, h, d, x).wait_send()
            for way in range(2):
                for s in range(1, 4):
                    cond, zo, to = ring_send(way, s)

                    @pl.when(cond)
                    def _():
                        ag_z(p, h, way, s, zo, to).wait_send()

        def left_zo(zo, carry):
            for h in range(2):
                ag_core(p, h, zo, k).wait_send()
            rs_core(p, zo).wait_send()
            for what in (RELAY, SUMMED, DIRECT):
                rs_y(p, zo, what).wait_send()

            @pl.when(zo > z)
            def _():
                rs_z(p, zo, z).wait_send()

            return carry

        lax.fori_loop(z, Z, left_zo, 0)
        return carry

    lax.fori_loop(0, 2, left, 0)
    collect(1)


def lay_out(held, out1, out2):
    for p, out in enumerate((out1, out2)):
        for h in range(2):
            for c in range(X):
                for t in range(2):
                    out[(c + 4 * t) * 64:(c + 4 * t + 1) * 64, h * 128:(h + 1) * 128] = held[
                        p, h, c, t * 64:(t + 1) * 64, :
                    ]


def per_device(density_panel, blocks, block_row, block_slot, requests):
    vmem = pl.BlockSpec(memory_space=pltpu.VMEM)
    dma = pltpu.SemaphoreType.DMA
    shape = jax.ShapeDtypeStruct((512, K), BF16)

    def pair(*dims):
        return [dma(dims), dma(dims)]

    scratch = [
        pltpu.VMEM((384, 4096), BF16),
        pltpu.VMEM((512, 8192), BF16),
        pltpu.VMEM((512, 768), BF16),
        pltpu.VMEM((512, 512), BF16),
        pltpu.VMEM((256, 512), BF16),
        pltpu.VMEM((2, 2, Z, C, 512, 128), BF16),
        pltpu.VMEM((2, 512, 128), F32),
        pltpu.VMEM((3, 2, X, 128, 128), BF16),
        pltpu.VMEM((Z, Y, K, 128), F32),
        pltpu.VMEM((2, Z, K, 512), BF16),
        pltpu.VMEM((2, Z, K, 512), BF16),
        pltpu.VMEM((2, Z, 3, K, 128), BF16),
        pltpu.VMEM((2, Z, 3, K, 128), BF16),
        pltpu.VMEM((2, Z, K, 128), BF16),
        pltpu.VMEM((2, Z, K, 128), BF16),
        pltpu.VMEM((K, 128), F32),
        pltpu.VMEM((2, 2, X, 128, 128), F32),
        pltpu.VMEM((2, 2, X - 1, 128, 128), F32),
        dma((4,)),
        *pair(2, 2, Y - 1),
        *pair(2, 2, 2, 3),
        *pair(2, 2),
        *pair(2, 2, Y - 1),
        *pair(2, 2, Z),
        *pair(2, Z),
        *pair(2, Z, 3),
        *pair(2, Z),
        *pair(2, 2, X - 1),
        *pair(2, 2, X - 1),
    ]
    held = pl.pallas_call(
        kernel,
        out_shape=jax.ShapeDtypeStruct((2, 2, X, 128, 128), BF16),
        in_specs=[vmem, pl.BlockSpec(memory_space=pl.ANY), vmem, vmem],
        out_specs=vmem,
        scratch_shapes=scratch,
        compiler_params=pltpu.CompilerParams(
            collective_id=0, has_side_effects=True, vmem_limit_bytes=60 * 1024 * 1024
        ),
    )(density_panel, blocks, block_row, block_slot)
    return pl.pallas_call(
        lay_out, out_shape=(shape, shape), in_specs=[vmem], out_specs=(vmem, vmem)
    )(held)


def solution(mesh):
    in_specs = (
        P("row", None),
        P(("row", "col"), None),
        P(("row", "col")),
        P(("row", "col")),
        P(("row", "col"), None),
    )
    out_specs = (P("row", None), P("row", None))
    return jax.shard_map(
        per_device, mesh=mesh, in_specs=in_specs, out_specs=out_specs, check_vma=False
    )
```
